32 devices in a mesh: dp: 4 (over y, x), seq: 8 (over z, core).
Axes of the slice: x: 2, y: 2, z: 4, core: 2. Of those that a mesh axis runs over, the one named last changes fastest.
Arguments:
- x_fwd: bfloat16 [16384, 1024], P(('dp', 'seq')), parts along dimension 0, may hold values from -6 to 6
- x_rev: bfloat16 [16384, 1024], P(('dp', 'seq')), parts along dimension 0, may hold values from -6 to 6
- gain: bfloat16 [1024], replicated, may hold values from 0.099609375 to 1.8984375
- w_qkv: bfloat16 [1024, 3072], replicated
Outputs:
- y_fwd: bfloat16 [16384, 1024], P(('dp', 'seq')), parts along dimension 0
- y_rev: bfloat16 [16384, 1024], P(('dp', 'seq')), parts along dimension 0
The draws below stay inside these ranges and needn't reach their ends.
There are 4 independent parts, one for each index of `dp`. The reference program is written for one: setup_inputs(seed, part) draws one part's arguments, and reference() takes and returns one part's arrays. A program takes and returns all parts, laid end to end along the dimension named above; an argument that names none is the same for every part. Nothing has to cross between parts.
All inputs are finite; a program needn't handle non-finite values.
Results may differ from the reference program's by a relative error of at most 0.012.
Values may be sent and summed in bfloat16 or wider, within the bound.
A program may use at most 128 MiB of HBM per device.

```python
import jax
import jax.numpy as jnp
from jax import lax

D = 1024
HEADS = 16
HEAD_DIM = 64
WINDOW = 512
ROWS = 512
LENGTH = 4096
N_SEQ = 8


def draw_w_qkv(key, part):
    inner = jax.random.fold_in(key, 11)
    first, second, third = jax.random.split(inner, 3)
    base_q = jax.random.normal(first, (D, D), jnp.float32)
    base_k = jax.random.normal(second, (D, D), jnp.float32)
    base_v = jax.random.normal(third, (D, D), jnp.float32)
    query = base_q * (1.4 * D ** (-0.5))
    keys = base_k * (1.4 * D ** (-0.5))
    values = base_v * (3.0 * D ** (-0.5))
    return jnp.concatenate([query, keys, values], axis=1).astype(jnp.bfloat16)


def block_levels(own_key, dims, pieces, least, top_value):
    def one(dim, parts):
        steps = jax.random.uniform(jax.random.fold_in(jax.random.fold_in(own_key, 6), dim), (parts,), jnp.float32, least / len(pieces), top_value / len(pieces))
        return jnp.repeat(jnp.exp(steps), dims[dim] // parts).reshape((-1,) + (1,) * (len(dims) - dim - 1))

    level = one(*pieces[0])
    for cut in pieces[1:]:
        level = level * one(*cut)
    return level


def centred(stream_key, extent, spread, bound, cuts=(), held_as=jnp.bfloat16):
    factor_of = block_levels(stream_key, extent, cuts, -0.22, 0.18) if cuts else 1.0
    drawn = jax.random.normal(stream_key, extent, jnp.float32) * spread * factor_of
    return jnp.minimum(jnp.maximum(drawn, -bound), bound).astype(held_as)


def setup_inputs(seed: int = 0, part: int = 0) -> dict:
    key_list = jax.random.split(jax.random.key(seed), 5)
    own_keys = jax.random.split(jax.random.fold_in(key_list[4], part), 5)
    return {
        "x_fwd": centred(own_keys[0], (LENGTH, D), 1.0, 6.0, ((0, 8),)),
        "x_rev": centred(own_keys[1], (LENGTH, D), 1.0, 6.0, ((0, 8),)),
        "gain": jnp.clip(1.0 + 0.18 * jax.random.normal(key_list[2], (D,), jnp.float32), 0.099609375, 1.8984375).astype(jnp.bfloat16),
        "w_qkv": draw_w_qkv(jax.random.fold_in(key_list[4], 71), part),
    }


def strand_attention(x, gain, w_qkv):
    xf = x.astype(jnp.float32)
    meansq = lax.optimization_barrier(jnp.mean(xf * xf, axis=-1, keepdims=True))
    normed = (xf * lax.rsqrt(meansq + 1e-06) * gain.astype(jnp.float32)).astype(jnp.bfloat16)
    qkv = jnp.dot(normed, w_qkv, preferred_element_type=jnp.float32).astype(jnp.bfloat16)
    query = qkv[:, :D]
    zeros = jnp.zeros((WINDOW, D), jnp.bfloat16)
    keys = jnp.concatenate([zeros, qkv[:, D:2 * D], zeros], axis=0)
    values = jnp.concatenate([zeros, qkv[:, 2 * D:], zeros], axis=0)
    scale = HEAD_DIM ** (-0.5)
    span = ROWS + 2 * WINDOW

    def block(index):
        start = (index * ROWS).astype(jnp.int32)
        qblock = lax.dynamic_slice_in_dim(query, start, ROWS, 0).astype(jnp.float32).reshape(ROWS, HEADS, HEAD_DIM)
        kblock = lax.dynamic_slice_in_dim(keys, start, span, 0).astype(jnp.float32).reshape(span, HEADS, HEAD_DIM)
        vblock = lax.dynamic_slice_in_dim(values, start, span, 0).astype(jnp.float32).reshape(span, HEADS, HEAD_DIM)
        scores = jnp.einsum('rhd,khd->hrk', qblock, kblock) * scale
        qpos = start + jnp.arange(ROWS, dtype=jnp.int32)
        kpos = start - WINDOW + jnp.arange(span, dtype=jnp.int32)
        inside = (jnp.abs(qpos[:, None] - kpos[None, :]) <= WINDOW) & (kpos[None, :] >= 0) & (kpos[None, :] < LENGTH)
        scores = jnp.where(inside[None], scores, -1e+30)
        top = lax.optimization_barrier(jnp.max(scores, axis=-1, keepdims=True))
        probs = jnp.exp(scores - top)
        denom = lax.optimization_barrier(jnp.sum(probs, axis=-1))
        rounded = lax.optimization_barrier(probs.astype(jnp.bfloat16)).astype(jnp.float32)
        out = jnp.einsum('hrk,khd->rhd', rounded, vblock) / jnp.transpose(denom)[:, :, None]
        return out.reshape(ROWS, D).astype(jnp.bfloat16)
    blocks = lax.map(block, jnp.arange(N_SEQ, dtype=jnp.int32))
    return blocks.reshape(LENGTH, D)

def reference(x_fwd, x_rev, gain, w_qkv):
    att_fwd = strand_attention(x_fwd, gain, w_qkv).astype(jnp.float32)
    att_rev = strand_attention(x_rev, gain, w_qkv).astype(jnp.float32)
    y_fwd = (att_fwd + att_rev[::-1, ::-1]).astype(jnp.bfloat16)
    y_rev = (att_rev + att_fwd[::-1, ::-1]).astype(jnp.bfloat16)
    return (y_fwd, y_rev)
```

```python
import functools
import math

import jax
import jax.numpy as jnp
from jax import lax
from jax.experimental import pallas as pl
from jax.experimental.pallas import tpu as pltpu
from jax.sharding import PartitionSpec as P

HEADS = 16
WINDOW = 512
BLOCK = 256
TILE = 512
LANES = 128
GROUPS = 4
VMEM_LIMIT = 48 * 1024 * 1024


def project_kernel(parts, gain_ref, *refs):
    x_refs = refs[:parts]
    w_ref, out_ref, hn_ref = refs[parts:]
    rows = x_refs[0].shape[0]

    @pl.when(pl.program_id(0) == 0)
    def _():
        gain = gain_ref[...].astype(jnp.float32)
        for part in range(parts):
            for start in range(0, rows, BLOCK):
                xf = x_refs[part][start:start + BLOCK, :].astype(jnp.float32)
                meansq = jnp.mean(xf * xf, axis=-1, keepdims=True)
                hn = xf * lax.rsqrt(meansq + 1e-06) * gain
                hn_ref[part * rows + start:part * rows + start + BLOCK, :] = hn.astype(jnp.bfloat16)

    out_ref[...] = jnp.dot(
        hn_ref[...], w_ref[...], preferred_element_type=jnp.float32
    ).astype(jnp.bfloat16)


def project(xs, gain, w, first_col):
    rows, width = xs[0].shape
    cols = w.shape[1] - first_col
    total = rows * len(xs)
    return pl.pallas_call(
        functools.partial(project_kernel, len(xs)),
        grid=(cols // TILE,),
        in_specs=[pl.BlockSpec((1, width), lambda j: (0, 0))]
        + [pl.BlockSpec((rows, width), lambda j: (0, 0)) for _ in xs]
        + [pl.BlockSpec((width, TILE), lambda j: (0, j + first_col // TILE))],
        out_specs=pl.BlockSpec((total, TILE), lambda j: (0, j)),
        out_shape=jax.ShapeDtypeStruct((total, cols), jnp.bfloat16),
        scratch_shapes=[pltpu.VMEM((total, width), jnp.bfloat16)],
        compiler_params=pltpu.CompilerParams(vmem_limit_bytes=VMEM_LIMIT),
        cost_estimate=pl.CostEstimate(
            flops=2 * total * width * cols,
            bytes_accessed=2 * (total * width + width * cols + total * cols),
            transcendentals=0,
        ),
    )(gain, *xs, w)


def attend_kernel(scale, bias_ref, flip_ref, q_ref, kl, ko, kr, vl, vo, vr, o_ref, mirror_ref, kx, vx):
    rows = q_ref.shape[0]
    span = 2 * WINDOW + BLOCK
    blocks = rows // BLOCK
    kx[:WINDOW, :] = kl[...]
    kx[WINDOW:WINDOW + rows, :] = ko[...]
    kx[WINDOW + rows:, :] = kr[...]
    start = 0
    for ref in (vl, vo, vr):
        v = ref[...]
        low = lax.broadcasted_iota(jnp.int32, v.shape, 1) < LANES // 2
        one = jnp.ones_like(v)
        vx[0, start:start + v.shape[0], :] = jnp.where(low, v, one)
        vx[1, start:start + v.shape[0], :] = jnp.where(low, one, v)
        start += v.shape[0]
    low = lax.broadcasted_iota(jnp.int32, (BLOCK, LANES), 1) < LANES // 2
    flip = flip_ref[...]
    for block in range(blocks):
        q = q_ref[block * BLOCK:(block + 1) * BLOCK, :]
        keys = kx[block * BLOCK:block * BLOCK + span, :]
        bias = bias_ref[block]
        outs = []
        for head in range(2):
            qh = jnp.where(low if head == 0 else ~low, q, jnp.zeros_like(q))
            s = lax.dot_general(
                qh, keys, (((1,), (1,)), ((), ())), preferred_element_type=jnp.float32
            )
            s = s * scale + bias
            top = jnp.max(s, axis=-1, keepdims=True)
            p = jnp.exp2(s - top).astype(jnp.bfloat16)
            outs.append(
                jnp.dot(
                    p,
                    vx[head, block * BLOCK:block * BLOCK + span, :],
                    preferred_element_type=jnp.float32,
                )
            )
        num = jnp.where(low, outs[0], outs[1])
        den = pltpu.roll(jnp.where(low, outs[1], outs[0]), LANES // 2, 1)
        a = (num / den).astype(jnp.bfloat16)
        o_ref[block * BLOCK:(block + 1) * BLOCK, :] = a
        turned = jnp.dot(flip, a, preferred_element_type=jnp.float32).astype(jnp.bfloat16)
        turned = jnp.dot(
            turned, flip[:LANES, BLOCK - LANES:], preferred_element_type=jnp.float32
        ).astype(jnp.bfloat16)
        other = blocks - 1 - block
        mirror_ref[other * BLOCK:(other + 1) * BLOCK, :] = turned


def attend(bias, flip, own, halo, group):
    rows = own.shape[0]
    width = own.shape[1] // 3
    pairs = width // LANES // GROUPS
    first = group * pairs
    per = width // LANES
    head_size = width // HEADS
    span = 2 * WINDOW + BLOCK
    blocks = rows // BLOCK
    scale = head_size ** (-0.5) * math.log2(math.e)

    def part(size, row, offset):
        return pl.BlockSpec((size, LANES), lambda j: (row, j + first + offset))

    return pl.pallas_call(
        functools.partial(attend_kernel, scale),
        grid=(pairs,),
        in_specs=[
            pl.BlockSpec(bias.shape, lambda j: (0, 0, 0)),
            pl.BlockSpec(flip.shape, lambda j: (0, 0)),
            part(rows, 0, 0),
            part(WINDOW, 0, 0),
            part(rows, 0, per),
            part(WINDOW, 1, 0),
            part(WINDOW, 0, per),
            part(rows, 0, 2 * per),
            part(WINDOW, 1, per),
        ],
        out_specs=[
            pl.BlockSpec((rows, LANES), lambda j: (0, j)),
            pl.BlockSpec((rows, LANES), lambda j: (0, pairs - 1 - j)),
        ],
        out_shape=[jax.ShapeDtypeStruct((rows, pairs * LANES), jnp.bfloat16)] * 2,
        scratch_shapes=[
            pltpu.VMEM((rows + 2 * WINDOW, LANES), jnp.bfloat16),
            pltpu.VMEM((2, rows + 2 * WINDOW, LANES), jnp.bfloat16),
        ],
        compiler_params=pltpu.CompilerParams(vmem_limit_bytes=VMEM_LIMIT),
        cost_estimate=pl.CostEstimate(
            flops=pairs * blocks * 8 * 2 * BLOCK * span * LANES,
            bytes_accessed=2 * pairs * LANES * (6 * rows + 4 * WINDOW) + bias.size * 4,
            transcendentals=pairs * 2 * rows * span,
        ),
    )(bias, flip, own, halo, own, halo, halo, own, halo)


def band(rows):
    span = 2 * WINDOW + BLOCK
    index = lax.axis_index("seq")
    low = jnp.where(index == 0, WINDOW, 0)
    high = jnp.where(index == lax.axis_size("seq") - 1, WINDOW + rows, 2 * WINDOW + rows)
    shape = (rows // BLOCK, BLOCK, span)
    base = lax.broadcasted_iota(jnp.int32, shape, 0) * BLOCK
    query = lax.broadcasted_iota(jnp.int32, shape, 1)
    key = lax.broadcasted_iota(jnp.int32, shape, 2)
    inside = (key >= query) & (key <= query + 2 * WINDOW) & (key + base >= low) & (key + base < high)
    return jnp.where(inside, 0.0, -1e30).astype(jnp.float32)


def per_device(x_fwd, x_rev, gain, w_qkv):
    rows = x_fwd.shape[0]
    count = lax.axis_size("seq")
    up = [(i, i + 1) for i in range(count - 1)]
    down = [(i + 1, i) for i in range(count - 1)]
    mirror = [(i, count - 1 - i) for i in range(count)]
    gain = gain.reshape(1, -1)

    halos = []
    for x in (x_fwd, x_rev):
        left = lax.ppermute(x[rows - WINDOW:], "seq", up)
        right = lax.ppermute(x[:WINDOW], "seq", down)
        halos.append((left, right))
    bias = band(rows)
    flip = jnp.flip(jnp.eye(BLOCK, dtype=jnp.bfloat16), axis=0)
    owns = [project((x,), gain, w_qkv, 0) for x in (x_fwd, x_rev)]
    near, far = [], []
    for strand in range(2):
        halo = project(halos[strand], gain, w_qkv, x_fwd.shape[1])
        for group in range(GROUPS):
            a, turned = attend(bias, flip, owns[strand], halo, group)
            near.append(a.astype(jnp.float32))
            far.append(lax.ppermute(turned, "seq", mirror).astype(jnp.float32))
    outs = []
    for strand in range(2):
        outs.append(
            jnp.concatenate(
                [
                    (near[strand * GROUPS + g] + far[(1 - strand) * GROUPS + GROUPS - 1 - g]).astype(jnp.bfloat16)
                    for g in range(GROUPS)
                ],
                axis=1,
            )
        )
    return tuple(outs)


def solution(mesh):
    in_specs = (P(("dp", "seq"), None), P(("dp", "seq"), None), P(), P())
    out_specs = (P(("dp", "seq"), None), P(("dp", "seq"), None))
    return jax.shard_map(
        per_device, mesh=mesh, in_specs=in_specs, out_specs=out_specs, check_vma=False
    )
```

```python
import functools
import math

import jax
import jax.numpy as jnp
from jax import lax
from jax.experimental import pallas as pl
from jax.experimental.pallas import tpu as pltpu
from jax.sharding import PartitionSpec as P

HEADS = 16
WINDOW = 512
BLOCK = 256
TILE = 256
LANES = 128
FAR = -1e30
MESH = pl.DeviceIdType.MESH


def kernel(
    count, scale, gain_ref, xf_ref, xr_ref, w_ref, y_ref,
    x_own, x_halo, w_vmem, hn, qkv, kx, vx, bias, band, flip, turned, arrived,
    load_sem, halo_send, halo_recv, turn_send, turn_recv,
):
    rows = xf_ref.shape[0]
    width = xf_ref.shape[1]
    pairs = width // LANES
    blocks = rows // BLOCK
    ext = rows + 2 * WINDOW
    span = 2 * WINDOW + BLOCK
    me = lax.axis_index("seq")
    left, right, across = me - 1, me + 1, count - 1 - me
    has_left, has_right = me > 0, me < count - 1
    x_refs = (xf_ref, xr_ref)

    loads = [
        pltpu.make_async_copy(xf_ref, x_own.at[0], load_sem.at[0]),
        pltpu.make_async_copy(w_ref, w_vmem, load_sem.at[2]),
        pltpu.make_async_copy(xr_ref, x_own.at[1], load_sem.at[1]),
    ]
    for copy in loads:
        copy.start()

    barrier = pltpu.get_barrier_semaphore()

    @pl.when(has_left)
    def _():
        pl.semaphore_signal(barrier, inc=1, device_id={"seq": left}, device_id_type=MESH)

    @pl.when(has_right)
    def _():
        pl.semaphore_signal(barrier, inc=1, device_id={"seq": right}, device_id_type=MESH)

    pl.semaphore_signal(barrier, inc=1, device_id={"seq": across}, device_id_type=MESH)
    pl.semaphore_wait(barrier, 1 + jnp.where(has_left, 1, 0) + jnp.where(has_right, 1, 0))

    def to_right(strand):
        return pltpu.make_async_remote_copy(
            src_ref=x_refs[strand].at[pl.ds(rows - WINDOW, WINDOW)],
            dst_ref=x_halo.at[strand, pl.ds(0, WINDOW)],
            send_sem=halo_send.at[strand, 0],
            recv_sem=halo_recv.at[strand, 0],
            device_id={"seq": right},
            device_id_type=MESH,
        )

    def to_left(strand):
        return pltpu.make_async_remote_copy(
            src_ref=x_refs[strand].at[pl.ds(0, WINDOW)],
            dst_ref=x_halo.at[strand, pl.ds(WINDOW, WINDOW)],
            send_sem=halo_send.at[strand, 1],
            recv_sem=halo_recv.at[strand, 1],
            device_id={"seq": left},
            device_id_type=MESH,
        )

    def send_halo(strand):
        @pl.when(has_right)
        def _():
            to_right(strand).start()

        @pl.when(has_left)
        def _():
            to_left(strand).start()

    def across_copy(strand, pair):
        return pltpu.make_async_remote_copy(
            src_ref=turned.at[strand, pair],
            dst_ref=arrived.at[strand, pair],
            send_sem=turn_send.at[strand, pair],
            recv_sem=turn_recv.at[strand, pair],
            device_id={"seq": across},
            device_id_type=MESH,
        )

    send_halo(0)

    @pl.when(jnp.logical_not(has_left))
    def _():
        x_halo[:, :WINDOW, :] = jnp.zeros((2, WINDOW, width), jnp.bfloat16)

    @pl.when(jnp.logical_not(has_right))
    def _():
        x_halo[:, WINDOW:, :] = jnp.zeros((2, WINDOW, width), jnp.bfloat16)

    row = lax.broadcasted_iota(jnp.int32, (BLOCK, BLOCK), 0)
    col = lax.broadcasted_iota(jnp.int32, (BLOCK, BLOCK), 1)
    band[0] = jnp.where(col >= row, 0.0, FAR)
    band[1] = jnp.where(col <= row, 0.0, FAR)
    flip[...] = jnp.where(col + row == BLOCK - 1, 1.0, 0.0).astype(jnp.bfloat16)
    key = lax.broadcasted_iota(jnp.int32, (ext, LANES), 0)
    first = jnp.where(has_left, 0, WINDOW)
    last = jnp.where(has_right, ext, WINDOW + rows)
    bias[...] = jnp.where((key >= first) & (key < last), 0.0, FAR).astype(jnp.bfloat16)

    def normalise(source, strand, total):
        def step(i, carry):
            at = pl.ds(pl.multiple_of(i * LANES, LANES), LANES)
            xf = source[strand, at, :].astype(jnp.float32)
            meansq = jnp.mean(xf * xf, axis=-1, keepdims=True)
            out = xf * lax.rsqrt(meansq + 1e-06) * gain_ref[...].astype(jnp.float32)
            hn[at, :] = out.astype(jnp.bfloat16)
            return carry

        lax.fori_loop(0, total // LANES, step, 0)

    def project_own(strand, carry):
        normalise(x_own, strand, rows)

        def step(j, carry):
            at = pl.ds(pl.multiple_of(j * TILE, TILE), TILE)
            out = jnp.dot(hn[:rows, :], w_vmem[:, at], preferred_element_type=jnp.float32)
            out = out * jnp.where(j < width // TILE, scale, 1.0)
            qkv[strand, WINDOW:WINDOW + rows, at] = out.astype(jnp.bfloat16)
            return carry

        return lax.fori_loop(0, 3 * width // TILE, step, carry)

    def project_halo(strand):
        normalise(x_halo, strand, 2 * WINDOW)

        def step(j, carry):
            at = pl.ds(pl.multiple_of(j * TILE, TILE), TILE)
            out = jnp.dot(hn[:2 * WINDOW, :], w_vmem[:, at], preferred_element_type=jnp.float32)
            out = out.astype(jnp.bfloat16)
            qkv[strand, :WINDOW, at] = out[:WINDOW]
            qkv[strand, WINDOW + rows:, at] = out[WINDOW:]
            return carry

        lax.fori_loop(width // TILE, 3 * width // TILE, step, 0)

    low = lax.broadcasted_iota(jnp.int32, (BLOCK, LANES), 1) < LANES // 2
    lane = lax.broadcasted_iota(jnp.int32, (BLOCK, LANES), 1)

    def attend(strand, pair):
        columns = [
            pl.ds(pl.multiple_of(pair * LANES + part * width, LANES), LANES) for part in range(3)
        ]

        def lay(i, carry):
            at = pl.ds(pl.multiple_of(i * BLOCK, BLOCK), BLOCK)
            k = qkv[strand, at, columns[1]]
            v = qkv[strand, at, columns[2]]
            side = bias[at, :]
            one = jnp.ones_like(v)
            kx[0, at, :] = jnp.where(low, k, side)
            kx[1, at, :] = jnp.where(low, side, k)
            vx[0, at, :] = jnp.where(low, v, one)
            vx[1, at, :] = jnp.where(low, one, v)
            return carry

        lax.fori_loop(0, ext // BLOCK, lay, 0)

        def block_step(block, carry):
            start = pl.multiple_of(block * BLOCK, BLOCK)
            q = qkv[strand, pl.ds(pl.multiple_of(WINDOW + start, BLOCK), BLOCK), columns[0]]
            outs = []
            for head in range(2):
                mark = jnp.where(lane == (LANES // 2 if head == 0 else 0), 1.0, 0.0).astype(jnp.bfloat16)
                qh = jnp.where(low if head == 0 else jnp.logical_not(low), q, mark)
                cuts = ((0, BLOCK), (BLOCK, 2 * WINDOW - BLOCK), (2 * WINDOW, BLOCK))
                scores = []
                for offset, size in cuts:
                    at = pl.ds(pl.multiple_of(start + offset, BLOCK), size)
                    scores.append(
                        lax.dot_general(
                            qh, kx[head, at, :], (((1,), (1,)), ((), ())),
                            preferred_element_type=jnp.float32,
                        )
                    )
                scores[0] = scores[0] + band[0]
                scores[2] = scores[2] + band[1]
                top = jnp.max(scores[1], axis=-1, keepdims=True)
                top = jnp.maximum(top, jnp.max(jnp.maximum(scores[0], scores[2]), axis=-1, keepdims=True))
                p = jnp.concatenate(
                    [jnp.exp2(s - top).astype(jnp.bfloat16) for s in scores], axis=1
                )
                outs.append(
                    jnp.dot(p, vx[head, pl.ds(start, span), :], preferred_element_type=jnp.float32)
                )
            num = jnp.where(low, outs[0], outs[1])
            den = pltpu.roll(jnp.where(low, outs[1], outs[0]), LANES // 2, 1)
            a = (num / den).astype(jnp.bfloat16)
            y_ref[strand, pl.ds(start, BLOCK), columns[0]] = a
            back = jnp.dot(flip[...], a, preferred_element_type=jnp.float32).astype(jnp.bfloat16)
            back = jnp.dot(
                back, flip[:LANES, BLOCK - LANES:], preferred_element_type=jnp.float32
            ).astype(jnp.bfloat16)
            other = pl.ds(pl.multiple_of((blocks - 1 - block) * BLOCK, BLOCK), BLOCK)
            turned[strand, pair, other, :] = back
            return carry

        lax.fori_loop(0, blocks, block_step, 0)
        across_copy(strand, pair).start()

    loads[0].wait()
    loads[1].wait()
    project_own(0, 0)
    send_halo(1)
    loads[2].wait()
    project_own(1, 0)

    def strand_step(strand):
        @pl.when(has_left)
        def _():
            to_right(strand).wait_recv()

        @pl.when(has_right)
        def _():
            to_left(strand).wait_recv()

        project_halo(strand)

        def pair_step(pair, carry):
            attend(strand, pair)
            return carry

        lax.fori_loop(0, pairs, pair_step, 0)

    strand_step(0)
    strand_step(1)

    def combine(strand):
        def step(pair, carry):
            across_copy(1 - strand, pair).wait_recv()
            columns = pl.ds(pl.multiple_of((pairs - 1 - pair) * LANES, LANES), LANES)
            near = y_ref[strand, :, columns].astype(jnp.float32)
            far = arrived[1 - strand, pair].astype(jnp.float32)
            y_ref[strand, :, columns] = (near + far).astype(jnp.bfloat16)
            return carry

        lax.fori_loop(0, pairs, step, 0)

    combine(1)
    combine(0)

    def finish(pair, carry):
        across_copy(0, pair).wait_send()
        across_copy(1, pair).wait_send()
        return carry

    lax.fori_loop(0, pairs, finish, 0)
    for strand in range(2):
        @pl.when(has_right)
        def _():
            to_right(strand).wait_send()

        @pl.when(has_left)
        def _():
            to_left(strand).wait_send()


def per_device(x_fwd, x_rev, gain, w_qkv):
    rows, width = x_fwd.shape
    count = lax.axis_size("seq")
    pairs = width // LANES
    ext = rows + 2 * WINDOW
    scale = (width // HEADS) ** (-0.5) * math.log2(math.e)
    anywhere = pl.BlockSpec(memory_space=pl.ANY)
    inside = pl.BlockSpec(memory_space=pltpu.VMEM)
    half = jnp.bfloat16
    y = pl.pallas_call(
        functools.partial(kernel, count, scale),
        in_specs=[inside, anywhere, anywhere, anywhere],
        out_specs=inside,
        out_shape=jax.ShapeDtypeStruct((2, rows, width), half),
        scratch_shapes=[
            pltpu.VMEM((2, rows, width), half),
            pltpu.VMEM((2, 2 * WINDOW, width), half),
            pltpu.VMEM((width, 3 * width), half),
            pltpu.VMEM((max(rows, 2 * WINDOW), width), half),
            pltpu.VMEM((2, ext, 3 * width), half),
            pltpu.VMEM((2, ext, LANES), half),
            pltpu.VMEM((2, ext, LANES), half),
            pltpu.VMEM((ext, LANES), half),
            pltpu.VMEM((2, BLOCK, BLOCK), jnp.float32),
            pltpu.VMEM((BLOCK, BLOCK), half),
            pltpu.VMEM((2, pairs, rows, LANES), half),
            pltpu.VMEM((2, pairs, rows, LANES), half),
            pltpu.SemaphoreType.DMA((3,)),
            pltpu.SemaphoreType.DMA((2, 2)),
            pltpu.SemaphoreType.DMA((2, 2)),
            pltpu.SemaphoreType.DMA((2, pairs)),
            pltpu.SemaphoreType.DMA((2, pairs)),
        ],
        compiler_params=pltpu.CompilerParams(
            collective_id=0, has_side_effects=True, vmem_limit_bytes=62 * 1024 * 1024
        ),
        cost_estimate=pl.CostEstimate(
            flops=2 * rows * width * 3 * width * 4,
            bytes_accessed=2 * (4 * rows * width + 3 * width * width),
            transcendentals=2 * HEADS * rows * (2 * WINDOW + BLOCK),
        ),
    )(gain.reshape(1, -1), x_fwd, x_rev, w_qkv)
    return y[0], y[1]


def solution(mesh):
    in_specs = (P(("dp", "seq"), None), P(("dp", "seq"), None), P(), P())
    out_specs = (P(("dp", "seq"), None), P(("dp", "seq"), None))
    return jax.shard_map(
        per_device, mesh=mesh, in_specs=in_specs, out_specs=out_specs, check_vma=False
    )
```

```python
import functools
import math

import jax
import jax.numpy as jnp
from jax import lax
from jax.experimental import pallas as pl
from jax.experimental.pallas import tpu as pltpu
from jax.sharding import PartitionSpec as P

HEADS = 16
WINDOW = 512
BLOCK = 256
TILE = 256
LANES = 128
FAR = -1e30
MESH = pl.DeviceIdType.MESH


def kernel(
    count, scale, gain_ref, xf_ref, xr_ref, w_ref, yf_ref, yr_ref,
    x_own, x_halo, w_vmem, hn, qkv, kx, vx, bias, band, flip, turned,
    load_sem, halo_send, halo_recv, cross_send, cross_recv, pass_send, pass_recv, back_send, back_recv,
):
    rows = xf_ref.shape[0]
    width = xf_ref.shape[1]
    pairs = width // LANES
    blocks = rows // BLOCK
    chunks = rows // LANES
    ext = rows + 2 * WINDOW
    span = 2 * WINDOW + BLOCK
    me = lax.axis_index("seq")
    left, right, across = me - 1, me + 1, count - 1 - me
    has_left, has_right = me > 0, me < count - 1
    no_left, no_right = me == 0, me == count - 1
    mid_low, mid_high = me == count // 2 - 1, me == count // 2
    pass_left = has_left & (me != count // 2)
    pass_right = has_right & (me != count // 2 - 1)

    load_x = pltpu.make_async_copy(xf_ref, x_own.at[0], load_sem.at[0])
    load_w = pltpu.make_async_copy(w_ref, w_vmem, load_sem.at[1])
    keep_low = pltpu.make_async_copy(
        xr_ref.at[pl.ds(rows - WINDOW, WINDOW)], x_halo.at[1, pl.ds(0, WINDOW)], load_sem.at[2]
    )
    keep_high = pltpu.make_async_copy(
        xr_ref.at[pl.ds(0, WINDOW)], x_halo.at[1, pl.ds(WINDOW, WINDOW)], load_sem.at[2]
    )
    load_x.start()
    load_w.start()

    barrier = pltpu.get_barrier_semaphore()

    @pl.when(has_left)
    def _():
        pl.semaphore_signal(barrier, inc=1, device_id={"seq": left}, device_id_type=MESH)

    @pl.when(has_right)
    def _():
        pl.semaphore_signal(barrier, inc=1, device_id={"seq": right}, device_id_type=MESH)

    pl.semaphore_signal(barrier, inc=1, device_id={"seq": across}, device_id_type=MESH)
    pl.semaphore_wait(barrier, 1 + jnp.where(has_left, 1, 0) + jnp.where(has_right, 1, 0))

    def remote(src, dst, send, recv, device):
        return pltpu.make_async_remote_copy(
            src_ref=src, dst_ref=dst, send_sem=send, recv_sem=recv,
            device_id={"seq": device}, device_id_type=MESH,
        )

    def to_right():
        return remote(
            xf_ref.at[pl.ds(rows - WINDOW, WINDOW)], x_halo.at[0, pl.ds(0, WINDOW)],
            halo_send.at[0], halo_recv.at[0], right,
        )

    def to_left():
        return remote(
            xf_ref.at[pl.ds(0, WINDOW)], x_halo.at[0, pl.ds(WINDOW, WINDOW)],
            halo_send.at[1], halo_recv.at[1], left,
        )

    def cross(chunk):
        at = pl.ds(chunk * LANES, LANES)
        return remote(xr_ref.at[at], x_own.at[1, at], cross_send.at[chunk], cross_recv.at[chunk], across)

    near_left = [c for c in range(chunks) if c * LANES >= rows - WINDOW]
    near_right = [c for c in range(chunks) if c * LANES < WINDOW]

    def hand_left(chunk):
        at = pl.ds(chunk * LANES, LANES)
        to = pl.ds(chunk * LANES - (rows - WINDOW), LANES)
        return remote(
            x_own.at[1, at], x_halo.at[1, to], pass_send.at[0, chunk], pass_recv.at[0, chunk], left
        )

    def hand_right(chunk):
        at = pl.ds(chunk * LANES, LANES)
        to = pl.ds(WINDOW + chunk * LANES, LANES)
        return remote(
            x_own.at[1, at], x_halo.at[1, to], pass_send.at[1, chunk], pass_recv.at[1, chunk], right
        )

    def columns_of(pair):
        return pl.ds(pl.multiple_of(pair * LANES, LANES), LANES)

    def send_back(pair):
        return remote(
            turned.at[pair], yr_ref.at[:, columns_of(pair)],
            back_send.at[pair], back_recv.at[pair], across,
        )

    pl.when(has_right)(lambda: to_right().start())
    pl.when(has_left)(lambda: to_left().start())
    pl.when(mid_low)(lambda: keep_low.start())
    pl.when(mid_high)(lambda: keep_high.start())

    @pl.when(no_left)
    def _():
        x_halo[0, :WINDOW, :] = jnp.zeros((WINDOW, width), jnp.bfloat16)
        x_halo[1, WINDOW:, :] = jnp.zeros((WINDOW, width), jnp.bfloat16)

    @pl.when(no_right)
    def _():
        x_halo[0, WINDOW:, :] = jnp.zeros((WINDOW, width), jnp.bfloat16)
        x_halo[1, :WINDOW, :] = jnp.zeros((WINDOW, width), jnp.bfloat16)

    row = lax.broadcasted_iota(jnp.int32, (BLOCK, BLOCK), 0)
    col = lax.broadcasted_iota(jnp.int32, (BLOCK, BLOCK), 1)
    band[0] = jnp.where(col >= row, 0.0, FAR)
    band[1] = jnp.where(col <= row, 0.0, FAR)
    flip[...] = jnp.where(col + row == BLOCK - 1, 1.0, 0.0).astype(jnp.bfloat16)
    key = lax.broadcasted_iota(jnp.int32, (ext, LANES), 0)
    for strand, (before, after) in enumerate(((has_left, has_right), (has_right, has_left))):
        first = jnp.where(before, 0, WINDOW)
        last = jnp.where(after, ext, WINDOW + rows)
        bias[strand] = jnp.where((key >= first) & (key < last), 0.0, FAR).astype(jnp.bfloat16)

    def project(source, strand, src, dst, total, first_tile):
        def normalise(i, carry):
            at = pl.ds(pl.multiple_of(src + i * LANES, LANES), LANES)
            xf = source[strand, at, :].astype(jnp.float32)
            meansq = jnp.mean(xf * xf, axis=-1, keepdims=True)
            out = xf * lax.rsqrt(meansq + 1e-06) * gain_ref[...].astype(jnp.float32)
            hn[pl.ds(pl.multiple_of(i * LANES, LANES), LANES), :] = out.astype(jnp.bfloat16)
            return carry

        lax.fori_loop(0, total // LANES, normalise, 0)

        def step(j, carry):
            at = pl.ds(pl.multiple_of(j * TILE, TILE), TILE)
            out = jnp.dot(hn[:total, :], w_vmem[:, at], preferred_element_type=jnp.float32)
            out = out * jnp.where(j < width // TILE, scale, 1.0)
            qkv[strand, pl.ds(pl.multiple_of(dst, LANES), total), at] = out.astype(jnp.bfloat16)
            return carry

        lax.fori_loop(first_tile, 3 * width // TILE, step, 0)

    def project_side(strand, side):
        project(x_halo, strand, side * WINDOW, side * (WINDOW + rows), WINDOW, width // TILE)

    lane = lax.broadcasted_iota(jnp.int32, (BLOCK, LANES), 1)
    low = lane < LANES // 2

    def attend(strand, pair):
        columns = [columns_of(pair + part * pairs) for part in range(3)]

        def lay(i, carry):
            at = pl.ds(pl.multiple_of(i * BLOCK, BLOCK), BLOCK)
            k = qkv[strand, at, columns[1]]
            v = qkv[strand, at, columns[2]]
            side = bias[strand, at, :]
            one = jnp.ones_like(v)
            kx[0, at, :] = jnp.where(low, k, side)
            kx[1, at, :] = jnp.where(low, side, k)
            vx[0, at, :] = jnp.where(low, v, one)
            vx[1, at, :] = jnp.where(low, one, v)
            return carry

        lax.fori_loop(0, ext // BLOCK, lay, 0)

        def block_step(block, carry):
            start = pl.multiple_of(block * BLOCK, BLOCK)
            here = pl.ds(start, BLOCK)
            q = qkv[strand, pl.ds(pl.multiple_of(WINDOW + start, BLOCK), BLOCK), columns[0]]
            cuts = ((0, BLOCK), (BLOCK, 2 * WINDOW - BLOCK), (2 * WINDOW, BLOCK))
            scores = []
            for head in range(2):
                mark = jnp.where(lane == (LANES // 2 if head == 0 else 0), 1.0, 0.0).astype(jnp.bfloat16)
                qh = jnp.where(low if head == 0 else jnp.logical_not(low), q, mark)
                scores.append(
                    [
                        lax.dot_general(
                            qh, kx[head, pl.ds(pl.multiple_of(start + offset, BLOCK), size), :],
                            (((1,), (1,)), ((), ())), preferred_element_type=jnp.float32,
                        )
                        for offset, size in cuts
                    ]
                )
            outs = []
            for head in range(2):
                one, two, three = scores[head]
                one = one + band[0]
                three = three + band[1]
                top = jnp.max(two, axis=-1, keepdims=True)
                top = jnp.maximum(top, jnp.max(jnp.maximum(one, three), axis=-1, keepdims=True))
                p = jnp.concatenate(
                    [jnp.exp2(s - top).astype(jnp.bfloat16) for s in (one, two, three)], axis=1
                )
                outs.append(
                    jnp.dot(p, vx[head, pl.ds(start, span), :], preferred_element_type=jnp.float32)
                )
            num = jnp.where(low, outs[0], outs[1])
            den = pltpu.roll(jnp.where(low, outs[1], outs[0]), LANES // 2, 1)
            a = (num / den).astype(jnp.bfloat16)
            back = jnp.dot(flip[...], a, preferred_element_type=jnp.float32).astype(jnp.bfloat16)
            back = jnp.dot(back, flip[:LANES, BLOCK - LANES:], preferred_element_type=jnp.float32)
            other = pl.ds(pl.multiple_of((blocks - 1 - block) * BLOCK, BLOCK), BLOCK)
            if strand == 0:
                yf_ref[here, columns[0]] = a
                turned[pairs - 1 - pair, other, :] = back.astype(jnp.bfloat16)
            else:
                total = a.astype(jnp.float32) + turned[pair, here, :].astype(jnp.float32)
                turned[pair, here, :] = total.astype(jnp.bfloat16)
                opposite = columns_of(pairs - 1 - pair)
                total = yf_ref[other, opposite].astype(jnp.float32) + back
                yf_ref[other, opposite] = total.astype(jnp.bfloat16)
            return carry

        lax.fori_loop(0, blocks, block_step, 0)
        if strand == 1:
            send_back(pair).start()

    def attend_all(strand):
        def pair_step(pair, carry):
            attend(strand, pair)
            return carry

        lax.fori_loop(0, pairs, pair_step, 0)

    load_x.wait()
    load_w.wait()
    project(x_own, 0, 0, WINDOW, rows, 0)
    pl.when(has_left)(lambda: to_right().wait_recv())
    pl.when(has_right)(lambda: to_left().wait_recv())
    for chunk in range(chunks):
        cross(chunk).start()
    project_side(0, 0)
    project_side(0, 1)
    attend_all(0)

    per = BLOCK // LANES
    for chunk in range(chunks):
        cross(chunk).wait_recv()
        if chunk in near_left:
            pl.when(pass_left)(lambda: hand_left(chunk).start())
        if chunk in near_right:
            pl.when(pass_right)(lambda: hand_right(chunk).start())
        if chunk % per == per - 1:
            at = (chunk + 1 - per) * LANES
            project(x_own, 1, at, WINDOW + at, BLOCK, 0)

    def wait_low():
        for chunk in near_left:
            pl.when(pass_right)(lambda: hand_left(chunk).wait_recv())
        pl.when(mid_low)(lambda: keep_low.wait())

    def wait_high():
        for chunk in near_right:
            pl.when(pass_left)(lambda: hand_right(chunk).wait_recv())
        pl.when(mid_high)(lambda: keep_high.wait())

    outer = jnp.where(me < count // 2, 1, 0)
    pl.when(me < count // 2)(wait_high)
    pl.when(me >= count // 2)(wait_low)
    project_side(1, outer)
    pl.when(me < count // 2)(wait_low)
    pl.when(me >= count // 2)(wait_high)
    project_side(1, 1 - outer)
    attend_all(1)

    def finish(pair, carry):
        send_back(pair).wait_recv()
        send_back(pair).wait_send()
        return carry

    lax.fori_loop(0, pairs, finish, 0)
    for chunk in range(chunks):
        cross(chunk).wait_send()
        if chunk in near_left:
            pl.when(pass_left)(lambda: hand_left(chunk).wait_send())
        if chunk in near_right:
            pl.when(pass_right)(lambda: hand_right(chunk).wait_send())
    pl.when(has_right)(lambda: to_right().wait_send())
    pl.when(has_left)(lambda: to_left().wait_send())


def per_device(x_fwd, x_rev, gain, w_qkv):
    rows, width = x_fwd.shape
    count = lax.axis_size("seq")
    pairs = width // LANES
    chunks = rows // LANES
    ext = rows + 2 * WINDOW
    scale = (width // HEADS) ** (-0.5) * math.log2(math.e)
    anywhere = pl.BlockSpec(memory_space=pl.ANY)
    inside = pl.BlockSpec(memory_space=pltpu.VMEM)
    half = jnp.bfloat16
    return pl.pallas_call(
        functools.partial(kernel, count, scale),
        in_specs=[inside, anywhere, anywhere, anywhere],
        out_specs=[inside, inside],
        out_shape=[jax.ShapeDtypeStruct((rows, width), half)] * 2,
        scratch_shapes=[
            pltpu.VMEM((2, rows, width), half),
            pltpu.VMEM((2, 2 * WINDOW, width), half),
            pltpu.VMEM((width, 3 * width), half),
            pltpu.VMEM((max(rows, WINDOW), width), half),
            pltpu.VMEM((2, ext, 3 * width), half),
            pltpu.VMEM((2, ext, LANES), half),
            pltpu.VMEM((2, ext, LANES), half),
            pltpu.VMEM((2, ext, LANES), half),
            pltpu.VMEM((2, BLOCK, BLOCK), jnp.float32),
            pltpu.VMEM((BLOCK, BLOCK), half),
            pltpu.VMEM((pairs, rows, LANES), half),
            pltpu.SemaphoreType.DMA((3,)),
            pltpu.SemaphoreType.DMA((2,)),
            pltpu.SemaphoreType.DMA((2,)),
            pltpu.SemaphoreType.DMA((chunks,)),
            pltpu.SemaphoreType.DMA((chunks,)),
            pltpu.SemaphoreType.DMA((2, chunks)),
            pltpu.SemaphoreType.DMA((2, chunks)),
            pltpu.SemaphoreType.DMA((pairs,)),
            pltpu.SemaphoreType.DMA((pairs,)),
        ],
        compiler_params=pltpu.CompilerParams(
            collective_id=0, has_side_effects=True, vmem_limit_bytes=62 * 1024 * 1024
        ),
        cost_estimate=pl.CostEstimate(
            flops=2 * rows * width * 3 * width * 4,
            bytes_accessed=2 * (4 * rows * width + 3 * width * width),
            transcendentals=2 * HEADS * rows * (2 * WINDOW + BLOCK),
        ),
    )(gain.reshape(1, -1), x_fwd, x_rev, w_qkv)


def solution(mesh):
    in_specs = (P(("dp", "seq"), None), P(("dp", "seq"), None), P(), P())
    out_specs = (P(("dp", "seq"), None), P(("dp", "seq"), None))
    return jax.shard_map(
        per_device, mesh=mesh, in_specs=in_specs, out_specs=out_specs, check_vma=False
    )
```

```python
import functools
import math

import jax
import jax.numpy as jnp
from jax import lax
from jax.experimental import pallas as pl
from jax.experimental.pallas import tpu as pltpu
from jax.sharding import PartitionSpec as P

HEADS = 16
WINDOW = 512
BLOCK = 256
TILE = 256
LANES = 128
FAR = -1e30
MESH = pl.DeviceIdType.MESH


def kernel(
    count, scale, gain_ref, xf_ref, xr_ref, w_ref, y_ref,
    x_own, x_halo, w_vmem, hn, qkv, qkv_group, kx, vx, bias, band, flip, turned,
    load_sem, halo_send, halo_recv, cross_send, cross_recv, pass_send, pass_recv, back_send, back_recv,
):
    rows = xf_ref.shape[0]
    width = xf_ref.shape[1]
    pairs = width // LANES
    blocks = rows // BLOCK
    chunks = rows // LANES
    ext = rows + 2 * WINDOW
    span = 2 * WINDOW + BLOCK
    me = lax.axis_index("seq")
    left, right, across = me - 1, me + 1, count - 1 - me
    has_left, has_right = me > 0, me < count - 1
    no_left, no_right = me == 0, me == count - 1
    mid_low, mid_high = me == count // 2 - 1, me == count // 2
    pass_left = has_left & (me != count // 2)
    pass_right = has_right & (me != count // 2 - 1)

    load_x = pltpu.make_async_copy(xf_ref, x_own.at[0], load_sem.at[0])
    load_w = pltpu.make_async_copy(w_ref, w_vmem, load_sem.at[1])
    keep_low = pltpu.make_async_copy(
        xr_ref.at[pl.ds(rows - WINDOW, WINDOW)], x_halo.at[1, pl.ds(0, WINDOW)], load_sem.at[2]
    )
    keep_high = pltpu.make_async_copy(
        xr_ref.at[pl.ds(0, WINDOW)], x_halo.at[1, pl.ds(WINDOW, WINDOW)], load_sem.at[2]
    )
    load_x.start()
    load_w.start()

    barrier = pltpu.get_barrier_semaphore()

    @pl.when(has_left)
    def _():
        pl.semaphore_signal(barrier, inc=1, device_id={"seq": left}, device_id_type=MESH)

    @pl.when(has_right)
    def _():
        pl.semaphore_signal(barrier, inc=1, device_id={"seq": right}, device_id_type=MESH)

    pl.semaphore_signal(barrier, inc=1, device_id={"seq": across}, device_id_type=MESH)
    pl.semaphore_wait(barrier, 1 + jnp.where(has_left, 1, 0) + jnp.where(has_right, 1, 0))

    def remote(src, dst, send, recv, device):
        return pltpu.make_async_remote_copy(
            src_ref=src, dst_ref=dst, send_sem=send, recv_sem=recv,
            device_id={"seq": device}, device_id_type=MESH,
        )

    def to_right():
        return remote(
            xf_ref.at[pl.ds(rows - WINDOW, WINDOW)], x_halo.at[0, pl.ds(0, WINDOW)],
            halo_send.at[0], halo_recv.at[0], right,
        )

    def to_left():
        return remote(
            xf_ref.at[pl.ds(0, WINDOW)], x_halo.at[0, pl.ds(WINDOW, WINDOW)],
            halo_send.at[1], halo_recv.at[1], left,
        )

    def cross(chunk):
        at = pl.ds(chunk * LANES, LANES)
        return remote(xr_ref.at[at], x_own.at[1, at], cross_send.at[chunk], cross_recv.at[chunk], across)

    near_left = [c for c in range(chunks) if c * LANES >= rows - WINDOW]
    near_right = [c for c in range(chunks) if c * LANES < WINDOW]

    def hand_left(chunk):
        at = pl.ds(chunk * LANES, LANES)
        to = pl.ds(chunk * LANES - (rows - WINDOW), LANES)
        return remote(
            x_own.at[1, at], x_halo.at[1, to], pass_send.at[0, chunk], pass_recv.at[0, chunk], left
        )

    def hand_right(chunk):
        at = pl.ds(chunk * LANES, LANES)
        to = pl.ds(WINDOW + chunk * LANES, LANES)
        return remote(
            x_own.at[1, at], x_halo.at[1, to], pass_send.at[1, chunk], pass_recv.at[1, chunk], right
        )

    def columns_of(pair):
        return pl.ds(pl.multiple_of(pair * LANES, LANES), LANES)

    def send_back(pair):
        return remote(
            turned.at[pair], y_ref.at[1, :, columns_of(pair)],
            back_send.at[pair], back_recv.at[pair], across,
        )

    pl.when(has_right)(lambda: to_right().start())
    pl.when(has_left)(lambda: to_left().start())
    pl.when(mid_low)(lambda: keep_low.start())
    pl.when(mid_high)(lambda: keep_high.start())

    @pl.when(no_left)
    def _():
        x_halo[0, :WINDOW, :] = jnp.zeros((WINDOW, width), jnp.bfloat16)
        x_halo[1, WINDOW:, :] = jnp.zeros((WINDOW, width), jnp.bfloat16)

    @pl.when(no_right)
    def _():
        x_halo[0, WINDOW:, :] = jnp.zeros((WINDOW, width), jnp.bfloat16)
        x_halo[1, :WINDOW, :] = jnp.zeros((WINDOW, width), jnp.bfloat16)

    row = lax.broadcasted_iota(jnp.int32, (BLOCK, BLOCK), 0)
    col = lax.broadcasted_iota(jnp.int32, (BLOCK, BLOCK), 1)
    band[0] = jnp.where(col >= row, 0.0, FAR)
    band[1] = jnp.where(col <= row, 0.0, FAR)
    flip[...] = jnp.where(col + row == BLOCK - 1, 1.0, 0.0).astype(jnp.bfloat16)
    key = lax.broadcasted_iota(jnp.int32, (LANES, ext), 1)
    for strand, (before, after) in enumerate(((has_left, has_right), (has_right, has_left))):
        first = jnp.where(before, 0, WINDOW)
        last = jnp.where(after, ext, WINDOW + rows)
        bias[strand] = jnp.where((key >= first) & (key < last), 0.0, FAR).astype(jnp.bfloat16)

    def normalise(source, strand, src, dst, total):
        def step(i, carry):
            at = pl.ds(pl.multiple_of(src + i * LANES, LANES), LANES)
            xf = source[strand, at, :].astype(jnp.float32)
            meansq = jnp.mean(xf * xf, axis=-1, keepdims=True)
            out = xf * lax.rsqrt(meansq + 1e-06) * gain_ref[...].astype(jnp.float32)
            hn[pl.ds(pl.multiple_of(dst + i * LANES, LANES), LANES), :] = out.astype(jnp.bfloat16)
            return carry

        lax.fori_loop(0, total // LANES, step, 0)

    tiles = width // TILE
    middle, ends = (WINDOW, rows), ((0, WINDOW), (WINDOW + rows, WINDOW))

    def project(out_ref, span_rows, tile, to):
        start, size = span_rows
        at = pl.ds(pl.multiple_of(tile * TILE, TILE), TILE)
        out = jnp.dot(hn[start:start + size, :], w_vmem[:, at], preferred_element_type=jnp.float32)
        out = out * jnp.where(tile < tiles, scale, 1.0)
        to = pl.ds(pl.multiple_of(to * TILE, TILE), TILE)
        out_ref[start:start + size, to] = out.astype(jnp.bfloat16)

    def project_fwd(span_rows, first_tile):
        def step(tile, carry):
            project(qkv, span_rows, tile, tile)
            return carry

        lax.fori_loop(first_tile, 3 * tiles, step, 0)

    def project_group(group):
        def own(part, carry):
            project(qkv_group, middle, part * tiles + group, part)
            return carry

        def halo(part, carry):
            for end in ends:
                project(qkv_group, end, part * tiles + group, part)
            return carry

        lax.fori_loop(0, 3, own, 0)
        lax.fori_loop(1, 3, halo, 0)

    lane = lax.broadcasted_iota(jnp.int32, (BLOCK, LANES), 1)
    low = lane < LANES // 2

    high_rows = lax.broadcasted_iota(jnp.int32, (LANES, BLOCK), 0) < LANES // 2

    def attend(strand, pair):
        if strand == 0:
            source, columns = qkv, [columns_of(pair + part * pairs) for part in range(3)]
        else:
            per = TILE // LANES
            source, columns = qkv_group, [columns_of(pair % per + part * per) for part in range(3)]
        own_columns = columns_of(pair)

        def lay(i, carry):
            at = pl.ds(pl.multiple_of(i * BLOCK, BLOCK), BLOCK)
            k = source[at, columns[1]].T
            v = source[at, columns[2]]
            side = bias[strand, :, at]
            one = jnp.ones_like(v)
            kx[0, :, at] = jnp.where(high_rows, k, side)
            kx[1, :, at] = jnp.where(high_rows, side, k)
            vx[0, at, :] = jnp.where(low, v, one)
            vx[1, at, :] = jnp.where(low, one, v)
            return carry

        lax.fori_loop(0, ext // BLOCK, lay, 0)
        cuts = ((0, BLOCK), (BLOCK, 2 * WINDOW - BLOCK), (2 * WINDOW, BLOCK))

        def score(start, head):
            q = source[pl.ds(pl.multiple_of(WINDOW + start, BLOCK), BLOCK), columns[0]]
            mark = jnp.where(lane == (LANES // 2 if head == 0 else 0), 1.0, 0.0).astype(jnp.bfloat16)
            qh = jnp.where(low if head == 0 else jnp.logical_not(low), q, mark)
            return [
                jnp.dot(
                    qh, kx[head, :, pl.ds(pl.multiple_of(start + offset, BLOCK), size)],
                    preferred_element_type=jnp.float32,
                )
                for offset, size in cuts
            ]

        def weigh(start, head, scores):
            one, two, three = scores
            one = one + band[0]
            three = three + band[1]
            top = jnp.max(two, axis=-1, keepdims=True)
            top = jnp.maximum(top, jnp.max(jnp.maximum(one, three), axis=-1, keepdims=True))
            p = jnp.concatenate(
                [jnp.exp2(s - top).astype(jnp.bfloat16) for s in (one, two, three)], axis=1
            )
            return jnp.dot(p, vx[head, pl.ds(start, span), :], preferred_element_type=jnp.float32)

        def store(block, start, outs):
            here = pl.ds(start, BLOCK)
            num = jnp.where(low, outs[0], outs[1])
            den = pltpu.roll(jnp.where(low, outs[1], outs[0]), LANES // 2, 1)
            a = (num / den).astype(jnp.bfloat16)
            back = jnp.dot(flip[...], a, preferred_element_type=jnp.float32).astype(jnp.bfloat16)
            back = jnp.dot(back, flip[:LANES, BLOCK - LANES:], preferred_element_type=jnp.float32)
            other = pl.ds(pl.multiple_of((blocks - 1 - block) * BLOCK, BLOCK), BLOCK)
            if strand == 0:
                y_ref[0, here, own_columns] = a
                turned[pairs - 1 - pair, other, :] = back.astype(jnp.bfloat16)
            else:
                total = a.astype(jnp.float32) + turned[pair, here, :].astype(jnp.float32)
                turned[pair, here, :] = total.astype(jnp.bfloat16)
                opposite = columns_of(pairs - 1 - pair)
                total = y_ref[0, other, opposite].astype(jnp.float32) + back
                y_ref[0, other, opposite] = total.astype(jnp.bfloat16)

        def blocks_step(step, carry):
            units = [
                (2 * step + sub, pl.multiple_of((2 * step + sub) * BLOCK, BLOCK), head)
                for sub in range(2) for head in range(2)
            ]
            ahead = score(*units[0][1:])
            outs = []
            for i, (block, start, head) in enumerate(units):
                scores = ahead
                if i + 1 < len(units):
                    ahead = score(*units[i + 1][1:])
                outs.append(weigh(start, head, scores))
                if head == 1:
                    store(block, start, outs[-2:])
            return carry

        lax.fori_loop(0, blocks // 2, blocks_step, 0)
        if strand == 1:
            send_back(pair).start()

    load_x.wait()
    load_w.wait()
    normalise(x_own, 0, 0, WINDOW, rows)
    project_fwd(middle, 0)
    pl.when(has_left)(lambda: to_right().wait_recv())
    pl.when(has_right)(lambda: to_left().wait_recv())
    for chunk in range(chunks):
        cross(chunk).start()
    normalise(x_halo, 0, 0, 0, WINDOW)
    normalise(x_halo, 0, WINDOW, WINDOW + rows, WINDOW)
    for end in ends:
        project_fwd(end, tiles)

    def fwd_step(pair, carry):
        attend(0, pair)
        return carry

    lax.fori_loop(0, pairs, fwd_step, 0)

    for chunk in range(chunks):
        cross(chunk).wait_recv()
        if chunk in near_left:
            pl.when(pass_left)(lambda: hand_left(chunk).start())
        if chunk in near_right:
            pl.when(pass_right)(lambda: hand_right(chunk).start())
        normalise(x_own, 1, chunk * LANES, WINDOW + chunk * LANES, LANES)

    def wait_low():
        for chunk in near_left:
            pl.when(pass_right)(lambda: hand_left(chunk).wait_recv())
        pl.when(mid_low)(lambda: keep_low.wait())

    def wait_high():
        for chunk in near_right:
            pl.when(pass_left)(lambda: hand_right(chunk).wait_recv())
        pl.when(mid_high)(lambda: keep_high.wait())

    outer = jnp.where(me < count // 2, 1, 0)
    inner = 1 - outer
    pl.when(me < count // 2)(wait_high)
    pl.when(me >= count // 2)(wait_low)
    normalise(x_halo, 1, outer * WINDOW, outer * (WINDOW + rows), WINDOW)
    pl.when(me < count // 2)(wait_low)
    pl.when(me >= count // 2)(wait_high)
    normalise(x_halo, 1, inner * WINDOW, inner * (WINDOW + rows), WINDOW)

    def rev_step(pair, carry):
        pl.when(pair % (TILE // LANES) == 0)(lambda: project_group(pair // (TILE // LANES)))
        attend(1, pair)
        return carry

    lax.fori_loop(0, pairs, rev_step, 0)

    def finish(pair, carry):
        send_back(pair).wait_recv()
        send_back(pair).wait_send()
        return carry

    lax.fori_loop(0, pairs, finish, 0)
    for chunk in range(chunks):
        cross(chunk).wait_send()
        if chunk in near_left:
            pl.when(pass_left)(lambda: hand_left(chunk).wait_send())
        if chunk in near_right:
            pl.when(pass_right)(lambda: hand_right(chunk).wait_send())
    pl.when(has_right)(lambda: to_right().wait_send())
    pl.when(has_left)(lambda: to_left().wait_send())


def per_device(x_fwd, x_rev, gain, w_qkv):
    rows, width = x_fwd.shape
    count = lax.axis_size("seq")
    pairs = width // LANES
    chunks = rows // LANES
    ext = rows + 2 * WINDOW
    scale = (width // HEADS) ** (-0.5) * math.log2(math.e)
    anywhere = pl.BlockSpec(memory_space=pl.ANY)
    inside = pl.BlockSpec(memory_space=pltpu.VMEM)
    half = jnp.bfloat16
    y = pl.pallas_call(
        functools.partial(kernel, count, scale),
        in_specs=[inside, anywhere, anywhere, anywhere],
        out_specs=inside,
        out_shape=jax.ShapeDtypeStruct((2, rows, width), half),
        scratch_shapes=[
            pltpu.VMEM((2, rows, width), half),
            pltpu.VMEM((2, 2 * WINDOW, width), half),
            pltpu.VMEM((width, 3 * width), half),
            pltpu.VMEM((ext, width), half),
            pltpu.VMEM((ext, 3 * width), half),
            pltpu.VMEM((ext, 3 * TILE), half),
            pltpu.VMEM((2, LANES, ext), half),
            pltpu.VMEM((2, ext, LANES), half),
            pltpu.VMEM((2, LANES, ext), half),
            pltpu.VMEM((2, BLOCK, BLOCK), jnp.float32),
            pltpu.VMEM((BLOCK, BLOCK), half),
            pltpu.VMEM((pairs, rows, LANES), half),
            pltpu.SemaphoreType.DMA((3,)),
            pltpu.SemaphoreType.DMA((2,)),
            pltpu.SemaphoreType.DMA((2,)),
            pltpu.SemaphoreType.DMA((chunks,)),
            pltpu.SemaphoreType.DMA((chunks,)),
            pltpu.SemaphoreType.DMA((2, chunks)),
            pltpu.SemaphoreType.DMA((2, chunks)),
            pltpu.SemaphoreType.DMA((pairs,)),
            pltpu.SemaphoreType.DMA((pairs,)),
        ],
        compiler_params=pltpu.CompilerParams(
            collective_id=0, has_side_effects=True, vmem_limit_bytes=62 * 1024 * 1024
        ),
        cost_estimate=pl.CostEstimate(
            flops=2 * rows * width * 3 * width * 4,
            bytes_accessed=2 * (4 * rows * width + 3 * width * width),
            transcendentals=2 * HEADS * rows * (2 * WINDOW + BLOCK),
        ),
    )(gain, x_fwd, x_rev, w_qkv)
    return y[0], y[1]


def solution(mesh):
    in_specs = (P(("dp", "seq"), None), P(("dp", "seq"), None), P(), P())
    out_specs = (P(("dp", "seq"), None), P(("dp", "seq"), None))
    return jax.shard_map(
        per_device, mesh=mesh, in_specs=in_specs, out_specs=out_specs, check_vma=False
    )
```

```python
import functools
import math

import jax
import jax.numpy as jnp
from jax import lax
from jax.experimental import pallas as pl
from jax.experimental.pallas import tpu as pltpu
from jax.sharding import PartitionSpec as P

HEADS = 16
WINDOW = 512
BLOCK = 256
TILE = 256
LANES = 128
FAR = -1e30
MESH = pl.DeviceIdType.MESH


def kernel(
    count, scale, gain_ref, xf_ref, xr_ref, w_ref, y_ref,
    x_own, x_halo, w_vmem, hn, qkv, kx, vx, bias, band, flip, turned,
    load_sem, halo_send, halo_recv, cross_send, cross_recv, pass_send, pass_recv, back_send, back_recv,
):
    rows = xf_ref.shape[0]
    width = xf_ref.shape[1]
    pairs = width // LANES
    blocks = rows // BLOCK
    chunks = rows // LANES
    ext = rows + 2 * WINDOW
    span = 2 * WINDOW + BLOCK
    me = lax.axis_index("seq")
    left, right, across = me - 1, me + 1, count - 1 - me
    has_left, has_right = me > 0, me < count - 1
    no_left, no_right = me == 0, me == count - 1
    mid_low, mid_high = me == count // 2 - 1, me == count // 2
    pass_left = has_left & (me != count // 2)
    pass_right = has_right & (me != count // 2 - 1)

    load_x = pltpu.make_async_copy(xf_ref, x_own.at[0], load_sem.at[0])
    load_w = pltpu.make_async_copy(w_ref, w_vmem, load_sem.at[1])
    keep_low = pltpu.make_async_copy(
        xr_ref.at[pl.ds(rows - WINDOW, WINDOW)], x_halo.at[1, pl.ds(0, WINDOW)], load_sem.at[2]
    )
    keep_high = pltpu.make_async_copy(
        xr_ref.at[pl.ds(0, WINDOW)], x_halo.at[1, pl.ds(WINDOW, WINDOW)], load_sem.at[2]
    )
    load_x.start()
    load_w.start()

    barrier = pltpu.get_barrier_semaphore()

    @pl.when(has_left)
    def _():
        pl.semaphore_signal(barrier, inc=1, device_id={"seq": left}, device_id_type=MESH)

    @pl.when(has_right)
    def _():
        pl.semaphore_signal(barrier, inc=1, device_id={"seq": right}, device_id_type=MESH)

    pl.semaphore_signal(barrier, inc=1, device_id={"seq": across}, device_id_type=MESH)
    pl.semaphore_wait(barrier, 1 + jnp.where(has_left, 1, 0) + jnp.where(has_right, 1, 0))

    def remote(src, dst, send, recv, device):
        return pltpu.make_async_remote_copy(
            src_ref=src, dst_ref=dst, send_sem=send, recv_sem=recv,
            device_id={"seq": device}, device_id_type=MESH,
        )

    def to_right():
        return remote(
            xf_ref.at[pl.ds(rows - WINDOW, WINDOW)], x_halo.at[0, pl.ds(0, WINDOW)],
            halo_send.at[0], halo_recv.at[0], right,
        )

    def to_left():
        return remote(
            xf_ref.at[pl.ds(0, WINDOW)], x_halo.at[0, pl.ds(WINDOW, WINDOW)],
            halo_send.at[1], halo_recv.at[1], left,
        )

    def cross(chunk):
        at = pl.ds(chunk * LANES, LANES)
        return remote(xr_ref.at[at], x_own.at[1, at], cross_send.at[chunk], cross_recv.at[chunk], across)

    near_left = [c for c in range(chunks) if c * LANES >= rows - WINDOW]
    near_right = [c for c in range(chunks) if c * LANES < WINDOW]

    def hand_left(chunk):
        at = pl.ds(chunk * LANES, LANES)
        to = pl.ds(chunk * LANES - (rows - WINDOW), LANES)
        return remote(
            x_own.at[1, at], x_halo.at[1, to], pass_send.at[0, chunk], pass_recv.at[0, chunk], left
        )

    def hand_right(chunk):
        at = pl.ds(chunk * LANES, LANES)
        to = pl.ds(WINDOW + chunk * LANES, LANES)
        return remote(
            x_own.at[1, at], x_halo.at[1, to], pass_send.at[1, chunk], pass_recv.at[1, chunk], right
        )

    def columns_of(pair):
        return pl.ds(pl.multiple_of(pair * LANES, LANES), LANES)

    def send_back(pair):
        return remote(
            turned.at[pair], y_ref.at[1, :, columns_of(pair)],
            back_send.at[pair], back_recv.at[pair], across,
        )

    pl.when(has_right)(lambda: to_right().start())
    pl.when(has_left)(lambda: to_left().start())
    pl.when(mid_low)(lambda: keep_low.start())
    pl.when(mid_high)(lambda: keep_high.start())

    @pl.when(no_left)
    def _():
        x_halo[0, :WINDOW, :] = jnp.zeros((WINDOW, width), jnp.bfloat16)
        x_halo[1, WINDOW:, :] = jnp.zeros((WINDOW, width), jnp.bfloat16)

    @pl.when(no_right)
    def _():
        x_halo[0, WINDOW:, :] = jnp.zeros((WINDOW, width), jnp.bfloat16)
        x_halo[1, :WINDOW, :] = jnp.zeros((WINDOW, width), jnp.bfloat16)

    row = lax.broadcasted_iota(jnp.int32, (BLOCK, BLOCK), 0)
    col = lax.broadcasted_iota(jnp.int32, (BLOCK, BLOCK), 1)
    band[0] = jnp.where(col >= row, 0.0, FAR)
    band[1] = jnp.where(col <= row, 0.0, FAR)
    flip[...] = jnp.where(col + row == BLOCK - 1, 1.0, 0.0).astype(jnp.bfloat16)
    key = lax.broadcasted_iota(jnp.int32, (LANES, ext), 1)
    for strand, (before, after) in enumerate(((has_left, has_right), (has_right, has_left))):
        first = jnp.where(before, 0, WINDOW)
        last = jnp.where(after, ext, WINDOW + rows)
        bias[strand] = jnp.where((key >= first) & (key < last), 0.0, FAR).astype(jnp.bfloat16)

    def normalise(source, strand, src, dst, total):
        def step(i, carry):
            at = pl.ds(pl.multiple_of(src + i * LANES, LANES), LANES)
            xf = source[strand, at, :].astype(jnp.float32)
            meansq = jnp.mean(xf * xf, axis=-1, keepdims=True)
            out = xf * lax.rsqrt(meansq + 1e-06) * gain_ref[...].astype(jnp.float32)
            hn[pl.ds(pl.multiple_of(dst + i * LANES, LANES), LANES), :] = out.astype(jnp.bfloat16)
            return carry

        lax.fori_loop(0, total // LANES, step, 0)

    tiles = width // TILE
    ends = ((0, WINDOW), (WINDOW + rows, WINDOW))

    def project(start, size, tile):
        at = pl.ds(pl.multiple_of(tile * TILE, TILE), TILE)
        here = pl.ds(pl.multiple_of(start, WINDOW), size)
        out = jnp.dot(hn[here, :], w_vmem[:, at], preferred_element_type=jnp.float32)
        out = out * jnp.where(tile < tiles, scale, 1.0)
        qkv[here, at] = out.astype(jnp.bfloat16)

    def project_all(start, size, first_tile):
        def step(tile, carry):
            project(start, size, tile)
            return carry

        lax.fori_loop(first_tile, 3 * tiles, step, 0)

    def project_group(start, size, first_part, group):
        def step(part, carry):
            project(start, size, part * tiles + group)
            return carry

        lax.fori_loop(first_part, 3, step, 0)

    lane = lax.broadcasted_iota(jnp.int32, (BLOCK, LANES), 1)
    low = lane < LANES // 2

    high_rows = lax.broadcasted_iota(jnp.int32, (LANES, BLOCK), 0) < LANES // 2

    def attend(strand, pair):
        columns = [columns_of(pair + part * pairs) for part in range(3)]
        own_columns = columns_of(pair)

        def lay(i, carry):
            at = pl.ds(pl.multiple_of(i * BLOCK, BLOCK), BLOCK)
            k = qkv[at, columns[1]].T
            v = qkv[at, columns[2]]
            side = bias[strand, :, at]
            one = jnp.ones_like(v)
            kx[0, :, at] = jnp.where(high_rows, k, side)
            kx[1, :, at] = jnp.where(high_rows, side, k)
            vx[0, at, :] = jnp.where(low, v, one)
            vx[1, at, :] = jnp.where(low, one, v)
            return carry

        lax.fori_loop(0, ext // BLOCK, lay, 0)
        cuts = ((0, BLOCK), (BLOCK, 2 * WINDOW - BLOCK), (2 * WINDOW, BLOCK))

        def score(start, head):
            q = qkv[pl.ds(pl.multiple_of(WINDOW + start, BLOCK), BLOCK), columns[0]]
            mark = jnp.where(lane == (LANES // 2 if head == 0 else 0), 1.0, 0.0).astype(jnp.bfloat16)
            qh = jnp.where(low if head == 0 else jnp.logical_not(low), q, mark)
            return [
                jnp.dot(
                    qh, kx[head, :, pl.ds(pl.multiple_of(start + offset, BLOCK), size)],
                    preferred_element_type=jnp.float32,
                )
                for offset, size in cuts
            ]

        def weigh(start, head, scores):
            one, two, three = scores
            one = one + band[0]
            three = three + band[1]
            top = jnp.max(two, axis=-1, keepdims=True)
            top = jnp.maximum(top, jnp.max(jnp.maximum(one, three), axis=-1, keepdims=True))
            p = jnp.concatenate(
                [jnp.exp2(s - top).astype(jnp.bfloat16) for s in (one, two, three)], axis=1
            )
            return jnp.dot(p, vx[head, pl.ds(start, span), :], preferred_element_type=jnp.float32)

        def store(block, start, outs):
            here = pl.ds(start, BLOCK)
            num = jnp.where(low, outs[0], outs[1])
            den = pltpu.roll(jnp.where(low, outs[1], outs[0]), LANES // 2, 1)
            a = (num / den).astype(jnp.bfloat16)
            back = jnp.dot(flip[...], a, preferred_element_type=jnp.float32).astype(jnp.bfloat16)
            back = jnp.dot(back, flip[:LANES, BLOCK - LANES:], preferred_element_type=jnp.float32)
            other = pl.ds(pl.multiple_of((blocks - 1 - block) * BLOCK, BLOCK), BLOCK)
            if strand == 0:
                y_ref[0, here, own_columns] = a
                turned[pairs - 1 - pair, other, :] = back.astype(jnp.bfloat16)
            else:
                total = a.astype(jnp.float32) + turned[pair, here, :].astype(jnp.float32)
                turned[pair, here, :] = total.astype(jnp.bfloat16)
                opposite = columns_of(pairs - 1 - pair)
                total = y_ref[0, other, opposite].astype(jnp.float32) + back
                y_ref[0, other, opposite] = total.astype(jnp.bfloat16)

        def blocks_step(step, carry):
            units = [
                (2 * step + sub, pl.multiple_of((2 * step + sub) * BLOCK, BLOCK), head)
                for sub in range(2) for head in range(2)
            ]
            ahead = score(*units[0][1:])
            outs = []
            for i, (block, start, head) in enumerate(units):
                scores = ahead
                if i + 1 < len(units):
                    ahead = score(*units[i + 1][1:])
                outs.append(weigh(start, head, scores))
                if head == 1:
                    store(block, start, outs[-2:])
            return carry

        lax.fori_loop(0, blocks // 2, blocks_step, 0)
        if strand == 1:
            send_back(pair).start()

    load_x.wait()
    load_w.wait()
    normalise(x_own, 0, 0, WINDOW, rows)
    project_all(WINDOW, rows, 0)
    pl.when(has_left)(lambda: to_right().wait_recv())
    pl.when(has_right)(lambda: to_left().wait_recv())
    for chunk in range(chunks):
        cross(chunk).start()
    normalise(x_halo, 0, 0, 0, WINDOW)
    normalise(x_halo, 0, WINDOW, WINDOW + rows, WINDOW)
    for end, size in ends:
        project_all(end, size, tiles)

    def fwd_step(pair, carry):
        attend(0, pair)
        return carry

    lax.fori_loop(0, pairs, fwd_step, 0)

    outer = jnp.where(me < count // 2, 1, 0)
    inner = 1 - outer
    outer_start, inner_start = outer * (WINDOW + rows), inner * (WINDOW + rows)
    middle = mid_low | mid_high
    edge = no_left | no_right
    early = ((me < count // 4) | (me >= count - count // 4)) & jnp.logical_not(edge)

    pl.when(mid_low)(lambda: keep_low.wait())
    pl.when(mid_high)(lambda: keep_high.wait())

    @pl.when(middle)
    def _():
        normalise(x_halo, 1, inner * WINDOW, inner_start, WINDOW)
        project_all(inner_start, WINDOW, tiles)

    for chunk in range(chunks):
        cross(chunk).wait_recv()
        if chunk in near_left:
            pl.when(pass_left)(lambda: hand_left(chunk).start())
        if chunk in near_right:
            pl.when(pass_right)(lambda: hand_right(chunk).start())
        normalise(x_own, 1, chunk * LANES, WINDOW + chunk * LANES, LANES)

    def wait_low():
        for chunk in near_left:
            pl.when(pass_right)(lambda: hand_left(chunk).wait_recv())

    def wait_high():
        for chunk in near_right:
            pl.when(pass_left)(lambda: hand_right(chunk).wait_recv())

    pl.when(early)(lambda: project_all(WINDOW, rows, 0))
    pl.when(me < count // 2)(wait_high)
    pl.when(me >= count // 2)(wait_low)

    @pl.when(jnp.logical_not(edge))
    def _():
        normalise(x_halo, 1, outer * WINDOW, outer_start, WINDOW)

    pl.when(early)(lambda: project_all(outer_start, WINDOW, tiles))
    pl.when(me < count // 2)(wait_low)
    pl.when(me >= count // 2)(wait_high)

    @pl.when(jnp.logical_not(middle))
    def _():
        normalise(x_halo, 1, inner * WINDOW, inner_start, WINDOW)

    def prepare(group):
        pl.when(jnp.logical_not(early))(lambda: project_group(WINDOW, rows, 0, group))
        pl.when(jnp.logical_not(early | edge))(lambda: project_group(outer_start, WINDOW, 1, group))
        pl.when(jnp.logical_not(middle))(lambda: project_group(inner_start, WINDOW, 1, group))

    def rev_step(pair, carry):
        pl.when(pair % (TILE // LANES) == 0)(lambda: prepare(pair // (TILE // LANES)))
        attend(1, pair)
        return carry

    lax.fori_loop(0, pairs, rev_step, 0)

    def finish(pair, carry):
        send_back(pair).wait_recv()
        send_back(pair).wait_send()
        return carry

    lax.fori_loop(0, pairs, finish, 0)
    for chunk in range(chunks):
        cross(chunk).wait_send()
        if chunk in near_left:
            pl.when(pass_left)(lambda: hand_left(chunk).wait_send())
        if chunk in near_right:
            pl.when(pass_right)(lambda: hand_right(chunk).wait_send())
    pl.when(has_right)(lambda: to_right().wait_send())
    pl.when(has_left)(lambda: to_left().wait_send())


def per_device(x_fwd, x_rev, gain, w_qkv):
    rows, width = x_fwd.shape
    count = lax.axis_size("seq")
    pairs = width // LANES
    chunks = rows // LANES
    ext = rows + 2 * WINDOW
    scale = (width // HEADS) ** (-0.5) * math.log2(math.e)
    anywhere = pl.BlockSpec(memory_space=pl.ANY)
    inside = pl.BlockSpec(memory_space=pltpu.VMEM)
    half = jnp.bfloat16
    y = pl.pallas_call(
        functools.partial(kernel, count, scale),
        in_specs=[inside, anywhere, anywhere, anywhere],
        out_specs=inside,
        out_shape=jax.ShapeDtypeStruct((2, rows, width), half),
        scratch_shapes=[
            pltpu.VMEM((2, rows, width), half),
            pltpu.VMEM((2, 2 * WINDOW, width), half),
            pltpu.VMEM((width, 3 * width), half),
            pltpu.VMEM((ext, width), half),
            pltpu.VMEM((ext, 3 * width), half),
            pltpu.VMEM((2, LANES, ext), half),
            pltpu.VMEM((2, ext, LANES), half),
            pltpu.VMEM((2, LANES, ext), half),
            pltpu.VMEM((2, BLOCK, BLOCK), jnp.float32),
            pltpu.VMEM((BLOCK, BLOCK), half),
            pltpu.VMEM((pairs, rows, LANES), half),
            pltpu.SemaphoreType.DMA((3,)),
            pltpu.SemaphoreType.DMA((2,)),
            pltpu.SemaphoreType.DMA((2,)),
            pltpu.SemaphoreType.DMA((chunks,)),
            pltpu.SemaphoreType.DMA((chunks,)),
            pltpu.SemaphoreType.DMA((2, chunks)),
            pltpu.SemaphoreType.DMA((2, chunks)),
            pltpu.SemaphoreType.DMA((pairs,)),
            pltpu.SemaphoreType.DMA((pairs,)),
        ],
        compiler_params=pltpu.CompilerParams(
            collective_id=0, has_side_effects=True, vmem_limit_bytes=62 * 1024 * 1024
        ),
        cost_estimate=pl.CostEstimate(
            flops=2 * rows * width * 3 * width * 4,
            bytes_accessed=2 * (4 * rows * width + 3 * width * width),
            transcendentals=2 * HEADS * rows * (2 * WINDOW + BLOCK),
        ),
    )(gain, x_fwd, x_rev, w_qkv)
    return y[0], y[1]


def solution(mesh):
    in_specs = (P(("dp", "seq"), None), P(("dp", "seq"), None), P(), P())
    out_specs = (P(("dp", "seq"), None), P(("dp", "seq"), None))
    return jax.shard_map(
        per_device, mesh=mesh, in_specs=in_specs, out_specs=out_specs, check_vma=False
    )
```

```python
import functools
import math

import jax
import jax.numpy as jnp
from jax import lax
from jax.experimental import pallas as pl
from jax.experimental.pallas import tpu as pltpu
from jax.sharding import PartitionSpec as P

HEADS = 16
WINDOW = 512
BLOCK = 256
TILE = 256
LANES = 128
FAR = -1e30
MESH = pl.DeviceIdType.MESH


def kernel(
    count, scale, gain_ref, xf_ref, xr_ref, w_ref, y_ref,
    x_own, x_halo, w_vmem, hn, qkv, kx, vx, bias, band, flip, turned,
    load_sem, halo_send, halo_recv, cross_send, cross_recv, pass_send, pass_recv, back_send, back_recv,
):
    rows = xf_ref.shape[0]
    width = xf_ref.shape[1]
    pairs = width // LANES
    blocks = rows // BLOCK
    chunks = rows // LANES
    ext = rows + 2 * WINDOW
    span = 2 * WINDOW + BLOCK
    me = lax.axis_index("seq")
    left, right, across = me - 1, me + 1, count - 1 - me
    has_left, has_right = me > 0, me < count - 1
    no_left, no_right = me == 0, me == count - 1
    mid_low, mid_high = me == count // 2 - 1, me == count // 2
    pass_left = has_left & (me != count // 2)
    pass_right = has_right & (me != count // 2 - 1)

    load_x = pltpu.make_async_copy(xf_ref, x_own.at[0], load_sem.at[0])
    load_w = pltpu.make_async_copy(w_ref, w_vmem, load_sem.at[1])
    keep_low = pltpu.make_async_copy(
        xr_ref.at[pl.ds(rows - WINDOW, WINDOW)], x_halo.at[1, pl.ds(0, WINDOW)], load_sem.at[2]
    )
    keep_high = pltpu.make_async_copy(
        xr_ref.at[pl.ds(0, WINDOW)], x_halo.at[1, pl.ds(WINDOW, WINDOW)], load_sem.at[2]
    )
    load_x.start()
    load_w.start()

    barrier = pltpu.get_barrier_semaphore()

    @pl.when(has_left)
    def _():
        pl.semaphore_signal(barrier, inc=1, device_id={"seq": left}, device_id_type=MESH)

    @pl.when(has_right)
    def _():
        pl.semaphore_signal(barrier, inc=1, device_id={"seq": right}, device_id_type=MESH)

    pl.semaphore_signal(barrier, inc=1, device_id={"seq": across}, device_id_type=MESH)
    pl.semaphore_wait(barrier, 1 + jnp.where(has_left, 1, 0) + jnp.where(has_right, 1, 0))

    def remote(src, dst, send, recv, device):
        return pltpu.make_async_remote_copy(
            src_ref=src, dst_ref=dst, send_sem=send, recv_sem=recv,
            device_id={"seq": device}, device_id_type=MESH,
        )

    def to_right():
        return remote(
            xf_ref.at[pl.ds(rows - WINDOW, WINDOW)], x_halo.at[0, pl.ds(0, WINDOW)],
            halo_send.at[0], halo_recv.at[0], right,
        )

    def to_left():
        return remote(
            xf_ref.at[pl.ds(0, WINDOW)], x_halo.at[0, pl.ds(WINDOW, WINDOW)],
            halo_send.at[1], halo_recv.at[1], left,
        )

    def cross(chunk):
        at = pl.ds(chunk * LANES, LANES)
        return remote(xr_ref.at[at], x_own.at[1, at], cross_send.at[chunk], cross_recv.at[chunk], across)

    near_left = [c for c in range(chunks) if c * LANES >= rows - WINDOW]
    near_right = [c for c in range(chunks) if c * LANES < WINDOW]

    def hand_left(chunk):
        at = pl.ds(chunk * LANES, LANES)
        to = pl.ds(chunk * LANES - (rows - WINDOW), LANES)
        return remote(
            x_own.at[1, at], x_halo.at[1, to], pass_send.at[0, chunk], pass_recv.at[0, chunk], left
        )

    def hand_right(chunk):
        at = pl.ds(chunk * LANES, LANES)
        to = pl.ds(WINDOW + chunk * LANES, LANES)
        return remote(
            x_own.at[1, at], x_halo.at[1, to], pass_send.at[1, chunk], pass_recv.at[1, chunk], right
        )

    def columns_of(pair):
        return pl.ds(pl.multiple_of(pair * LANES, LANES), LANES)

    def send_back(pair):
        return remote(
            turned.at[pair], y_ref.at[1, :, columns_of(pair)],
            back_send.at[pair], back_recv.at[pair], across,
        )

    pl.when(has_right)(lambda: to_right().start())
    pl.when(has_left)(lambda: to_left().start())
    pl.when(mid_low)(lambda: keep_low.start())
    pl.when(mid_high)(lambda: keep_high.start())

    @pl.when(no_left)
    def _():
        x_halo[0, :WINDOW, :] = jnp.zeros((WINDOW, width), jnp.bfloat16)
        x_halo[1, WINDOW:, :] = jnp.zeros((WINDOW, width), jnp.bfloat16)

    @pl.when(no_right)
    def _():
        x_halo[0, WINDOW:, :] = jnp.zeros((WINDOW, width), jnp.bfloat16)
        x_halo[1, :WINDOW, :] = jnp.zeros((WINDOW, width), jnp.bfloat16)

    row = lax.broadcasted_iota(jnp.int32, (BLOCK, BLOCK), 0)
    col = lax.broadcasted_iota(jnp.int32, (BLOCK, BLOCK), 1)
    band[0] = jnp.where(col >= row, 0.0, FAR)
    band[1] = jnp.where(col <= row, 0.0, FAR)
    flip[...] = jnp.where(col + row == BLOCK - 1, 1.0, 0.0).astype(jnp.bfloat16)
    key = lax.broadcasted_iota(jnp.int32, (LANES, ext), 1)
    for strand, (before, after) in enumerate(((has_left, has_right), (has_right, has_left))):
        first = jnp.where(before, 0, WINDOW)
        last = jnp.where(after, ext, WINDOW + rows)
        bias[strand] = jnp.where((key >= first) & (key < last), 0.0, FAR).astype(jnp.bfloat16)

    def normalise(source, strand, src, dst, total):
        def step(i, carry):
            at = pl.ds(pl.multiple_of(src + i * LANES, LANES), LANES)
            xf = source[strand, at, :].astype(jnp.float32)
            meansq = jnp.mean(xf * xf, axis=-1, keepdims=True)
            out = xf * lax.rsqrt(meansq + 1e-06) * gain_ref[...].astype(jnp.float32)
            hn[pl.ds(pl.multiple_of(dst + i * LANES, LANES), LANES), :] = out.astype(jnp.bfloat16)
            return carry

        lax.fori_loop(0, total // LANES, step, 0)

    tiles = width // TILE
    ends = ((0, WINDOW), (WINDOW + rows, WINDOW))

    def project(start, size, tile):
        at = pl.ds(pl.multiple_of(tile * TILE, TILE), TILE)
        here = pl.ds(pl.multiple_of(start, BLOCK), size)
        out = jnp.dot(hn[here, :], w_vmem[:, at], preferred_element_type=jnp.float32)
        out = out * jnp.where(tile < tiles, scale, 1.0)
        qkv[here, at] = out.astype(jnp.bfloat16)

    def project_all(start, size, first_tile):
        def step(tile, carry):
            project(start, size, tile)
            return carry

        lax.fori_loop(first_tile, 3 * tiles, step, 0)

    def project_group(start, size, first_part, group):
        def step(part, carry):
            project(start, size, part * tiles + group)
            return carry

        lax.fori_loop(first_part, 3, step, 0)

    lane = lax.broadcasted_iota(jnp.int32, (BLOCK, LANES), 1)
    low = lane < LANES // 2

    high_rows = lax.broadcasted_iota(jnp.int32, (LANES, BLOCK), 0) < LANES // 2

    def attend(strand, pair):
        columns = [columns_of(pair + part * pairs) for part in range(3)]
        own_columns = columns_of(pair)

        for i in range(ext // BLOCK):
            at = pl.ds(i * BLOCK, BLOCK)
            k = qkv[at, columns[1]].T
            v = qkv[at, columns[2]]
            side = bias[strand, :, at]
            one = jnp.ones_like(v)
            kx[0, :, at] = jnp.where(high_rows, k, side)
            kx[1, :, at] = jnp.where(high_rows, side, k)
            vx[0, at, :] = jnp.where(low, v, one)
            vx[1, at, :] = jnp.where(low, one, v)

        cuts = ((0, BLOCK), (BLOCK, 2 * WINDOW - BLOCK), (2 * WINDOW, BLOCK))

        def score(start, head):
            q = qkv[pl.ds(pl.multiple_of(WINDOW + start, BLOCK), BLOCK), columns[0]]
            mark = jnp.where(lane == (LANES // 2 if head == 0 else 0), 1.0, 0.0).astype(jnp.bfloat16)
            qh = jnp.where(low if head == 0 else jnp.logical_not(low), q, mark)
            return [
                jnp.dot(
                    qh, kx[head, :, pl.ds(pl.multiple_of(start + offset, BLOCK), size)],
                    preferred_element_type=jnp.float32,
                )
                for offset, size in cuts
            ]

        def weigh(start, head, scores):
            one, two, three = scores
            one = one + band[0]
            three = three + band[1]
            top = jnp.max(two, axis=-1, keepdims=True)
            top = jnp.maximum(top, jnp.max(jnp.maximum(one, three), axis=-1, keepdims=True))
            p = jnp.concatenate(
                [jnp.exp2(s - top).astype(jnp.bfloat16) for s in (one, two, three)], axis=1
            )
            return jnp.dot(p, vx[head, pl.ds(start, span), :], preferred_element_type=jnp.float32)

        def store(start, outs):
            here = pl.ds(start, BLOCK)
            num = jnp.where(low, outs[0], outs[1])
            den = pltpu.roll(jnp.where(low, outs[1], outs[0]), LANES // 2, 1)
            a = (num / den).astype(jnp.bfloat16)
            if strand == 0:
                y_ref[0, here, own_columns] = a
            else:
                x_own[0, here, own_columns] = a
                total = a.astype(jnp.float32) + turned[pair, here, :].astype(jnp.float32)
                turned[pair, here, :] = total.astype(jnp.bfloat16)

        def blocks_step(step, carry):
            units = [
                (pl.multiple_of((2 * step + sub) * BLOCK, BLOCK), head)
                for sub in range(2) for head in range(2)
            ]
            ahead = score(*units[0])
            outs = []
            for i, (start, head) in enumerate(units):
                scores = ahead
                if i + 1 < len(units):
                    ahead = score(*units[i + 1])
                outs.append(weigh(start, head, scores))
                if head == 1:
                    store(start, outs[-2:])
            return carry

        if blocks == 2:
            blocks_step(0, 0)
        else:
            lax.fori_loop(0, blocks // 2, blocks_step, 0)
        if strand == 1:
            send_back(pair).start()

    def reverse(source_ref, take):
        for group in range(tiles):
            for block in range(blocks):
                a = source_ref[0, block * BLOCK:(block + 1) * BLOCK, group * TILE:(group + 1) * TILE]
                back = jnp.dot(flip[...], a, preferred_element_type=jnp.float32).astype(jnp.bfloat16)
                back = jnp.dot(back, flip[...], preferred_element_type=jnp.float32)
                other = (blocks - 1 - block) * BLOCK
                take(slice(other, other + BLOCK), tiles - 1 - group, back)

    def keep_turned(at, group, back):
        per = TILE // LANES
        for part in range(per):
            piece = back[:, part * LANES:(part + 1) * LANES]
            turned[group * per + part, at, :] = piece.astype(jnp.bfloat16)

    def add_turned(at, group, back):
        cols = slice(group * TILE, (group + 1) * TILE)
        y_ref[0, at, cols] = (y_ref[0, at, cols].astype(jnp.float32) + back).astype(jnp.bfloat16)

    load_x.wait()
    load_w.wait()
    normalise(x_own, 0, 0, WINDOW, rows)
    project_all(WINDOW, rows, 0)
    pl.when(has_left)(lambda: to_right().wait_recv())
    pl.when(has_right)(lambda: to_left().wait_recv())
    for chunk in range(chunks):
        cross(chunk).start()
    normalise(x_halo, 0, 0, 0, WINDOW)
    normalise(x_halo, 0, WINDOW, WINDOW + rows, WINDOW)
    for end, size in ends:
        project_all(end, size, tiles)

    def fwd_step(pair, carry):
        attend(0, pair)
        return carry

    lax.fori_loop(0, pairs, fwd_step, 0)
    reverse(y_ref, keep_turned)

    outer = jnp.where(me < count // 2, 1, 0)
    inner = 1 - outer
    outer_start, inner_start = outer * (WINDOW + rows), inner * (WINDOW + rows)
    middle = mid_low | mid_high
    edge = no_left | no_right
    early = ((me < count // 4) | (me >= count - count // 4)) & jnp.logical_not(edge)

    pl.when(mid_low)(lambda: keep_low.wait())
    pl.when(mid_high)(lambda: keep_high.wait())

    @pl.when(middle)
    def _():
        normalise(x_halo, 1, inner * WINDOW, inner_start, WINDOW)
        project_all(inner_start, WINDOW, tiles)

    for chunk in range(chunks):
        cross(chunk).wait_recv()
        if chunk in near_left:
            pl.when(pass_left)(lambda: hand_left(chunk).start())
        if chunk in near_right:
            pl.when(pass_right)(lambda: hand_right(chunk).start())
        normalise(x_own, 1, chunk * LANES, WINDOW + chunk * LANES, LANES)
        if chunk == chunks // 2 - 1:
            project_all(WINDOW, rows // 2, 0)

    def wait_low():
        for chunk in near_left:
            pl.when(pass_right)(lambda: hand_left(chunk).wait_recv())

    def wait_high():
        for chunk in near_right:
            pl.when(pass_left)(lambda: hand_right(chunk).wait_recv())

    pl.when(early)(lambda: project_all(WINDOW + rows // 2, rows // 2, 0))
    pl.when(me < count // 2)(wait_high)
    pl.when(me >= count // 2)(wait_low)

    @pl.when(jnp.logical_not(edge))
    def _():
        normalise(x_halo, 1, outer * WINDOW, outer_start, WINDOW)

    pl.when(early)(lambda: project_all(outer_start, WINDOW, tiles))
    pl.when(me < count // 2)(wait_low)
    pl.when(me >= count // 2)(wait_high)

    @pl.when(jnp.logical_not(middle))
    def _():
        normalise(x_halo, 1, inner * WINDOW, inner_start, WINDOW)

    def prepare(group):
        pl.when(jnp.logical_not(early))(lambda: project_group(WINDOW + rows // 2, rows // 2, 0, group))
        pl.when(jnp.logical_not(early | edge))(lambda: project_group(outer_start, WINDOW, 1, group))
        pl.when(jnp.logical_not(middle))(lambda: project_group(inner_start, WINDOW, 1, group))

    def rev_step(pair, carry):
        pl.when(pair % (TILE // LANES) == 0)(lambda: prepare(pair // (TILE // LANES)))
        attend(1, pair)
        return carry

    lax.fori_loop(0, pairs, rev_step, 0)
    reverse(x_own, add_turned)

    def finish(pair, carry):
        send_back(pair).wait_recv()
        send_back(pair).wait_send()
        return carry

    lax.fori_loop(0, pairs, finish, 0)
    for chunk in range(chunks):
        cross(chunk).wait_send()
        if chunk in near_left:
            pl.when(pass_left)(lambda: hand_left(chunk).wait_send())
        if chunk in near_right:
            pl.when(pass_right)(lambda: hand_right(chunk).wait_send())
    pl.when(has_right)(lambda: to_right().wait_send())
    pl.when(has_left)(lambda: to_left().wait_send())


def per_device(x_fwd, x_rev, gain, w_qkv):
    rows, width = x_fwd.shape
    count = lax.axis_size("seq")
    pairs = width // LANES
    chunks = rows // LANES
    ext = rows + 2 * WINDOW
    scale = (width // HEADS) ** (-0.5) * math.log2(math.e)
    anywhere = pl.BlockSpec(memory_space=pl.ANY)
    inside = pl.BlockSpec(memory_space=pltpu.VMEM)
    half = jnp.bfloat16
    y = pl.pallas_call(
        functools.partial(kernel, count, scale),
        in_specs=[inside, anywhere, anywhere, anywhere],
        out_specs=inside,
        out_shape=jax.ShapeDtypeStruct((2, rows, width), half),
        scratch_shapes=[
            pltpu.VMEM((2, rows, width), half),
            pltpu.VMEM((2, 2 * WINDOW, width), half),
            pltpu.VMEM((width, 3 * width), half),
            pltpu.VMEM((ext, width), half),
            pltpu.VMEM((ext, 3 * width), half),
            pltpu.VMEM((2, LANES, ext), half),
            pltpu.VMEM((2, ext, LANES), half),
            pltpu.VMEM((2, LANES, ext), half),
            pltpu.VMEM((2, BLOCK, BLOCK), jnp.float32),
            pltpu.VMEM((BLOCK, BLOCK), half),
            pltpu.VMEM((pairs, rows, LANES), half),
            pltpu.SemaphoreType.DMA((3,)),
            pltpu.SemaphoreType.DMA((2,)),
            pltpu.SemaphoreType.DMA((2,)),
            pltpu.SemaphoreType.DMA((chunks,)),
            pltpu.SemaphoreType.DMA((chunks,)),
            pltpu.SemaphoreType.DMA((2, chunks)),
            pltpu.SemaphoreType.DMA((2, chunks)),
            pltpu.SemaphoreType.DMA((pairs,)),
            pltpu.SemaphoreType.DMA((pairs,)),
        ],
        compiler_params=pltpu.CompilerParams(
            collective_id=0, has_side_effects=True, vmem_limit_bytes=62 * 1024 * 1024
        ),
        cost_estimate=pl.CostEstimate(
            flops=2 * rows * width * 3 * width * 4,
            bytes_accessed=2 * (4 * rows * width + 3 * width * width),
            transcendentals=2 * HEADS * rows * (2 * WINDOW + BLOCK),
        ),
    )(gain, x_fwd, x_rev, w_qkv)
    return y[0], y[1]


def solution(mesh):
    in_specs = (P(("dp", "seq"), None), P(("dp", "seq"), None), P(), P())
    out_specs = (P(("dp", "seq"), None), P(("dp", "seq"), None))
    return jax.shard_map(
        per_device, mesh=mesh, in_specs=in_specs, out_specs=out_specs, check_vma=False
    )
```

```python
import functools
import math

import jax
import jax.numpy as jnp
from jax import lax
from jax.experimental import pallas as pl
from jax.experimental.pallas import tpu as pltpu
from jax.sharding import PartitionSpec as P

HEADS = 16
WINDOW = 512
BLOCK = 256
TILE = 256
LANES = 128
FAR = -1e30
MESH = pl.DeviceIdType.MESH


def kernel(
    count, scale, gain_ref, xf_ref, xr_ref, w_ref, y_ref,
    x_own, x_halo, w_vmem, hn, qkv, kx, vx, bias, band, flip, turned,
    load_sem, halo_send, halo_recv, cross_send, cross_recv, pass_send, pass_recv, back_send, back_recv,
):
    rows = xf_ref.shape[0]
    width = xf_ref.shape[1]
    pairs = width // LANES
    blocks = rows // BLOCK
    chunks = rows // LANES
    ext = rows + 2 * WINDOW
    span = 2 * WINDOW + BLOCK
    me = lax.axis_index("seq")
    left, right, across = me - 1, me + 1, count - 1 - me
    has_left, has_right = me > 0, me < count - 1
    no_left, no_right = me == 0, me == count - 1
    mid_low, mid_high = me == count // 2 - 1, me == count // 2
    pass_left = has_left & (me != count // 2)
    pass_right = has_right & (me != count // 2 - 1)

    load_x = pltpu.make_async_copy(xf_ref, x_own.at[0], load_sem.at[0])
    load_w = pltpu.make_async_copy(w_ref, w_vmem, load_sem.at[1])
    keep_low = pltpu.make_async_copy(
        xr_ref.at[pl.ds(rows - WINDOW, WINDOW)], x_halo.at[1, pl.ds(0, WINDOW)], load_sem.at[2]
    )
    keep_high = pltpu.make_async_copy(
        xr_ref.at[pl.ds(0, WINDOW)], x_halo.at[1, pl.ds(WINDOW, WINDOW)], load_sem.at[2]
    )
    load_x.start()
    load_w.start()

    barrier = pltpu.get_barrier_semaphore()

    @pl.when(has_left)
    def _():
        pl.semaphore_signal(barrier, inc=1, device_id={"seq": left}, device_id_type=MESH)

    @pl.when(has_right)
    def _():
        pl.semaphore_signal(barrier, inc=1, device_id={"seq": right}, device_id_type=MESH)

    pl.semaphore_signal(barrier, inc=1, device_id={"seq": across}, device_id_type=MESH)
    pl.semaphore_wait(barrier, 1 + jnp.where(has_left, 1, 0) + jnp.where(has_right, 1, 0))

    def remote(src, dst, send, recv, device):
        return pltpu.make_async_remote_copy(
            src_ref=src, dst_ref=dst, send_sem=send, recv_sem=recv,
            device_id={"seq": device}, device_id_type=MESH,
        )

    def to_right():
        return remote(
            xf_ref.at[pl.ds(rows - WINDOW, WINDOW)], x_halo.at[0, pl.ds(0, WINDOW)],
            halo_send.at[0], halo_recv.at[0], right,
        )

    def to_left():
        return remote(
            xf_ref.at[pl.ds(0, WINDOW)], x_halo.at[0, pl.ds(WINDOW, WINDOW)],
            halo_send.at[1], halo_recv.at[1], left,
        )

    def cross(chunk):
        at = pl.ds(chunk * LANES, LANES)
        return remote(xr_ref.at[at], x_own.at[1, at], cross_send.at[chunk], cross_recv.at[chunk], across)

    near_left = [c for c in range(chunks) if c * LANES >= rows - WINDOW]
    near_right = [c for c in range(chunks) if c * LANES < WINDOW]

    def hand_left(chunk):
        at = pl.ds(chunk * LANES, LANES)
        to = pl.ds(chunk * LANES - (rows - WINDOW), LANES)
        return remote(
            x_own.at[1, at], x_halo.at[1, to], pass_send.at[0, chunk], pass_recv.at[0, chunk], left
        )

    def hand_right(chunk):
        at = pl.ds(chunk * LANES, LANES)
        to = pl.ds(WINDOW + chunk * LANES, LANES)
        return remote(
            x_own.at[1, at], x_halo.at[1, to], pass_send.at[1, chunk], pass_recv.at[1, chunk], right
        )

    def columns_of(pair):
        return pl.ds(pl.multiple_of(pair * LANES, LANES), LANES)

    def send_back(pair):
        return remote(
            turned.at[pair], y_ref.at[1, :, columns_of(pair)],
            back_send.at[pair], back_recv.at[pair], across,
        )

    pl.when(has_right)(lambda: to_right().start())
    pl.when(has_left)(lambda: to_left().start())
    pl.when(mid_low)(lambda: keep_low.start())
    pl.when(mid_high)(lambda: keep_high.start())

    @pl.when(no_left)
    def _():
        x_halo[0, :WINDOW, :] = jnp.zeros((WINDOW, width), jnp.bfloat16)
        x_halo[1, WINDOW:, :] = jnp.zeros((WINDOW, width), jnp.bfloat16)

    @pl.when(no_right)
    def _():
        x_halo[0, WINDOW:, :] = jnp.zeros((WINDOW, width), jnp.bfloat16)
        x_halo[1, :WINDOW, :] = jnp.zeros((WINDOW, width), jnp.bfloat16)

    row = lax.broadcasted_iota(jnp.int32, (BLOCK, BLOCK), 0)
    col = lax.broadcasted_iota(jnp.int32, (BLOCK, BLOCK), 1)
    band[0] = jnp.where(col >= row, 0.0, FAR)
    band[1] = jnp.where(col <= row, 0.0, FAR)
    flip[...] = jnp.where(col + row == BLOCK - 1, 1.0, 0.0).astype(jnp.bfloat16)
    key = lax.broadcasted_iota(jnp.int32, (LANES, ext), 1)
    for strand, (before, after) in enumerate(((has_left, has_right), (has_right, has_left))):
        first = jnp.where(before, 0, WINDOW)
        last = jnp.where(after, ext, WINDOW + rows)
        bias[strand] = jnp.where((key >= first) & (key < last), 0.0, FAR).astype(jnp.bfloat16)

    def normalise(source, strand, src, dst, total):
        def step(i, carry):
            at = pl.ds(pl.multiple_of(src + i * LANES, LANES), LANES)
            xf = source[strand, at, :].astype(jnp.float32)
            meansq = jnp.mean(xf * xf, axis=-1, keepdims=True)
            out = xf * lax.rsqrt(meansq + 1e-06) * gain_ref[...].astype(jnp.float32)
            hn[pl.ds(pl.multiple_of(dst + i * LANES, LANES), LANES), :] = out.astype(jnp.bfloat16)
            return carry

        lax.fori_loop(0, total // LANES, step, 0)

    tiles = width // TILE
    ends = ((0, WINDOW), (WINDOW + rows, WINDOW))

    def project(start, size, tile):
        at = pl.ds(pl.multiple_of(tile * TILE, TILE), TILE)
        here = pl.ds(pl.multiple_of(start, BLOCK), size)
        out = jnp.dot(hn[here, :], w_vmem[:, at], preferred_element_type=jnp.float32)
        out = out * jnp.where(tile < tiles, scale, 1.0)
        qkv[here, at] = out.astype(jnp.bfloat16)

    def project_all(start, size, first_tile):
        def step(tile, carry):
            project(start, size, tile)
            return carry

        lax.fori_loop(first_tile, 3 * tiles, step, 0)

    def project_group(start, size, first_part, group):
        def step(part, carry):
            project(start, size, part * tiles + group)
            return carry

        lax.fori_loop(first_part, 3, step, 0)

    lane = lax.broadcasted_iota(jnp.int32, (BLOCK, LANES), 1)
    low = lane < LANES // 2

    high_rows = lax.broadcasted_iota(jnp.int32, (LANES, BLOCK), 0) < LANES // 2

    def attend(strand, pair):
        columns = [columns_of(pair + part * pairs) for part in range(3)]
        own_columns = columns_of(pair)

        for i in range(ext // BLOCK):
            at = pl.ds(i * BLOCK, BLOCK)
            k = qkv[at, columns[1]].T
            v = qkv[at, columns[2]]
            side = bias[strand, :, at]
            one = jnp.ones_like(v)
            kx[0, :, at] = jnp.where(high_rows, k, side)
            kx[1, :, at] = jnp.where(high_rows, side, k)
            vx[0, at, :] = jnp.where(low, v, one)
            vx[1, at, :] = jnp.where(low, one, v)

        cuts = ((0, BLOCK), (BLOCK, 2 * WINDOW - BLOCK), (2 * WINDOW, BLOCK))

        def score(start, head):
            q = qkv[pl.ds(pl.multiple_of(WINDOW + start, BLOCK), BLOCK), columns[0]]
            mark = jnp.where(lane == (LANES // 2 if head == 0 else 0), 1.0, 0.0).astype(jnp.bfloat16)
            qh = jnp.where(low if head == 0 else jnp.logical_not(low), q, mark)
            return [
                jnp.dot(
                    qh, kx[head, :, pl.ds(pl.multiple_of(start + offset, BLOCK), size)],
                    preferred_element_type=jnp.float32,
                )
                for offset, size in cuts
            ]

        def weigh(start, head, scores):
            one, two, three = scores
            one = one + band[0]
            three = three + band[1]
            top = jnp.max(two, axis=-1, keepdims=True)
            top = jnp.maximum(top, jnp.max(jnp.maximum(one, three), axis=-1, keepdims=True))
            p = jnp.concatenate(
                [jnp.exp2(s - top).astype(jnp.bfloat16) for s in (one, two, three)], axis=1
            )
            return jnp.dot(p, vx[head, pl.ds(start, span), :], preferred_element_type=jnp.float32)

        def store(start, outs):
            here = pl.ds(start, BLOCK)
            num = jnp.where(low, outs[0], outs[1])
            den = pltpu.roll(jnp.where(low, outs[1], outs[0]), LANES // 2, 1)
            a = (num / den).astype(jnp.bfloat16)
            if strand == 0:
                y_ref[0, here, own_columns] = a
            else:
                x_own[0, here, own_columns] = a
                total = a.astype(jnp.float32) + turned[pair, here, :].astype(jnp.float32)
                turned[pair, here, :] = total.astype(jnp.bfloat16)

        def blocks_step(step, carry):
            units = [
                (pl.multiple_of((2 * step + sub) * BLOCK, BLOCK), head)
                for sub in range(2) for head in range(2)
            ]
            ahead = score(*units[0])
            outs = []
            for i, (start, head) in enumerate(units):
                scores = ahead
                if i + 1 < len(units):
                    ahead = score(*units[i + 1])
                outs.append(weigh(start, head, scores))
                if head == 1:
                    store(start, outs[-2:])
            return carry

        if blocks == 2:
            blocks_step(0, 0)
        else:
            lax.fori_loop(0, blocks // 2, blocks_step, 0)
        if strand == 1:
            send_back(pair).start()

    def reverse(source_ref, take):
        for group in range(tiles):
            for block in range(blocks):
                a = source_ref[0, block * BLOCK:(block + 1) * BLOCK, group * TILE:(group + 1) * TILE]
                back = jnp.dot(flip[...], a, preferred_element_type=jnp.float32).astype(jnp.bfloat16)
                back = jnp.dot(back, flip[...], preferred_element_type=jnp.float32)
                other = (blocks - 1 - block) * BLOCK
                take(slice(other, other + BLOCK), tiles - 1 - group, back)

    def keep_turned(at, group, back):
        per = TILE // LANES
        for part in range(per):
            piece = back[:, part * LANES:(part + 1) * LANES]
            turned[group * per + part, at, :] = piece.astype(jnp.bfloat16)

    def add_turned(at, group, back):
        cols = slice(group * TILE, (group + 1) * TILE)
        y_ref[0, at, cols] = (y_ref[0, at, cols].astype(jnp.float32) + back).astype(jnp.bfloat16)

    load_x.wait()
    load_w.wait()
    normalise(x_own, 0, 0, WINDOW, rows)
    project_all(WINDOW, rows, 0)
    pl.when(has_left)(lambda: to_right().wait_recv())
    pl.when(has_right)(lambda: to_left().wait_recv())
    middle = mid_low | mid_high

    def start_cross():
        for chunk in range(chunks):
            cross(chunk).start()

    pl.when(jnp.logical_not(middle))(start_cross)
    normalise(x_halo, 0, 0, 0, WINDOW)
    normalise(x_halo, 0, WINDOW, WINDOW + rows, WINDOW)
    for end, size in ends:
        project_all(end, size, tiles)

    def fwd_step(pair, carry):
        pl.when(middle & (pair == pairs - 1))(start_cross)
        attend(0, pair)
        return carry

    lax.fori_loop(0, pairs, fwd_step, 0)
    reverse(y_ref, keep_turned)

    outer = jnp.where(me < count // 2, 1, 0)
    inner = 1 - outer
    outer_start, inner_start = outer * (WINDOW + rows), inner * (WINDOW + rows)
    edge = no_left | no_right
    early = jnp.logical_not(edge | middle)

    pl.when(mid_low)(lambda: keep_low.wait())
    pl.when(mid_high)(lambda: keep_high.wait())

    @pl.when(middle)
    def _():
        normalise(x_halo, 1, inner * WINDOW, inner_start, WINDOW)
        project_all(inner_start, WINDOW, tiles)

    for chunk in range(chunks):
        cross(chunk).wait_recv()
        if chunk in near_left:
            pl.when(pass_left)(lambda: hand_left(chunk).start())
        if chunk in near_right:
            pl.when(pass_right)(lambda: hand_right(chunk).start())
        normalise(x_own, 1, chunk * LANES, WINDOW + chunk * LANES, LANES)
        if chunk == chunks // 2 - 1:
            project_all(WINDOW, rows // 2, 0)

    def wait_low():
        for chunk in near_left:
            pl.when(pass_right)(lambda: hand_left(chunk).wait_recv())

    def wait_high():
        for chunk in near_right:
            pl.when(pass_left)(lambda: hand_right(chunk).wait_recv())

    pl.when(early)(lambda: project_all(WINDOW + rows // 2, rows // 2, 0))
    pl.when(me < count // 2)(wait_high)
    pl.when(me >= count // 2)(wait_low)

    @pl.when(jnp.logical_not(edge))
    def _():
        normalise(x_halo, 1, outer * WINDOW, outer_start, WINDOW)

    pl.when(early)(lambda: project_all(outer_start, WINDOW, tiles))
    pl.when(me < count // 2)(wait_low)
    pl.when(me >= count // 2)(wait_high)

    @pl.when(jnp.logical_not(middle))
    def _():
        normalise(x_halo, 1, inner * WINDOW, inner_start, WINDOW)

    def prepare(group):
        pl.when(jnp.logical_not(early))(lambda: project_group(WINDOW + rows // 2, rows // 2, 0, group))
        pl.when(jnp.logical_not(early | edge))(lambda: project_group(outer_start, WINDOW, 1, group))
        pl.when(jnp.logical_not(middle))(lambda: project_group(inner_start, WINDOW, 1, group))

    def rev_step(pair, carry):
        pl.when(pair % (TILE // LANES) == 0)(lambda: prepare(pair // (TILE // LANES)))
        attend(1, pair)
        return carry

    lax.fori_loop(0, pairs, rev_step, 0)
    reverse(x_own, add_turned)

    def finish(pair, carry):
        send_back(pair).wait_recv()
        send_back(pair).wait_send()
        return carry

    lax.fori_loop(0, pairs, finish, 0)
    for chunk in range(chunks):
        cross(chunk).wait_send()
        if chunk in near_left:
            pl.when(pass_left)(lambda: hand_left(chunk).wait_send())
        if chunk in near_right:
            pl.when(pass_right)(lambda: hand_right(chunk).wait_send())
    pl.when(has_right)(lambda: to_right().wait_send())
    pl.when(has_left)(lambda: to_left().wait_send())


def per_device(x_fwd, x_rev, gain, w_qkv):
    rows, width = x_fwd.shape
    count = lax.axis_size("seq")
    pairs = width // LANES
    chunks = rows // LANES
    ext = rows + 2 * WINDOW
    scale = (width // HEADS) ** (-0.5) * math.log2(math.e)
    anywhere = pl.BlockSpec(memory_space=pl.ANY)
    inside = pl.BlockSpec(memory_space=pltpu.VMEM)
    half = jnp.bfloat16
    y = pl.pallas_call(
        functools.partial(kernel, count, scale),
        in_specs=[inside, anywhere, anywhere, anywhere],
        out_specs=inside,
        out_shape=jax.ShapeDtypeStruct((2, rows, width), half),
        scratch_shapes=[
            pltpu.VMEM((2, rows, width), half),
            pltpu.VMEM((2, 2 * WINDOW, width), half),
            pltpu.VMEM((width, 3 * width), half),
            pltpu.VMEM((ext, width), half),
            pltpu.VMEM((ext, 3 * width), half),
            pltpu.VMEM((2, LANES, ext), half),
            pltpu.VMEM((2, ext, LANES), half),
            pltpu.VMEM((2, LANES, ext), half),
            pltpu.VMEM((2, BLOCK, BLOCK), jnp.float32),
            pltpu.VMEM((BLOCK, BLOCK), half),
            pltpu.VMEM((pairs, rows, LANES), half),
            pltpu.SemaphoreType.DMA((3,)),
            pltpu.SemaphoreType.DMA((2,)),
            pltpu.SemaphoreType.DMA((2,)),
            pltpu.SemaphoreType.DMA((chunks,)),
            pltpu.SemaphoreType.DMA((chunks,)),
            pltpu.SemaphoreType.DMA((2, chunks)),
            pltpu.SemaphoreType.DMA((2, chunks)),
            pltpu.SemaphoreType.DMA((pairs,)),
            pltpu.SemaphoreType.DMA((pairs,)),
        ],
        compiler_params=pltpu.CompilerParams(
            collective_id=0, has_side_effects=True, vmem_limit_bytes=62 * 1024 * 1024
        ),
        cost_estimate=pl.CostEstimate(
            flops=2 * rows * width * 3 * width * 4,
            bytes_accessed=2 * (4 * rows * width + 3 * width * width),
            transcendentals=2 * HEADS * rows * (2 * WINDOW + BLOCK),
        ),
    )(gain, x_fwd, x_rev, w_qkv)
    return y[0], y[1]


def solution(mesh):
    in_specs = (P(("dp", "seq"), None), P(("dp", "seq"), None), P(), P())
    out_specs = (P(("dp", "seq"), None), P(("dp", "seq"), None))
    return jax.shard_map(
        per_device, mesh=mesh, in_specs=in_specs, out_specs=out_specs, check_vma=False
    )
```
